128 devices in a mesh: wide: 8 (over z_hi, y), seq: 16 (over z_lo, x, core).
Axes of the slice: x: 4, y: 4, z: 4 (z_hi: 2, z_lo: 2; z = z_hi * 2 + z_lo), core: 2. Of those that a mesh axis runs over, the one named last changes fastest.
Arguments:
- tokens: bfloat16 [98304, 512], P(('wide', 'seq')), may hold values from -6 to 6
- user_ids: int32 [98304], P(('wide', 'seq')), may hold values from 0 to 31, never falling along the last dimension, each value on 1 to 6144 neighbouring positions
- in_gain: float32 [512], replicated, may hold values from 0.5 to 1.5
- out_gain: float32 [512], replicated, may hold values from 0.5 to 1.5
- w_in: bfloat16 [512, 2048], replicated, may hold values from -0.25 to 0.25
- w_out: bfloat16 [512, 512], replicated, may hold values from -0.25 to 0.25
- cotangent: bfloat16 [98304, 512], P(('wide', 'seq')), may hold values from -6 to 6
Outputs:
- layer_out: bfloat16 [98304, 512], P(('wide', 'seq'))
- grad_tokens: bfloat16 [98304, 512], P(('wide', 'seq'))
- grad_w_in: float32 [512, 2048], replicated
- grad_w_out: float32 [512, 512], replicated
The draws below stay inside these ranges and needn't reach their ends.
Inputs may be any that keep to these rules, and one draw needn't show every extreme that they name: `user_ids`: never falling along the pack; each user holds 1 to 6144 consecutive events, one exactly 6144, and every user number occurs.
All inputs are finite; a program needn't handle non-finite values.
Results may differ from the reference program's by a relative error of at most 0.0084.
Values may be sent and summed in bfloat16 or wider, within the bound.
No kernel may reach another device: no remote copies, remote signals or barrier semaphores. Data moves between devices by JAX's collectives and lax.ppermute only.
A program may use at most 192 MiB of HBM per device.

```python
import math
import jax
import jax.numpy as jnp
import numpy as np
from jax import lax

D = 512
HEADS = 4
HEAD_DIM = 128
SPAN = 2
TOK_DEV = 768
TOKENS = 98304
USERS = 32
MAXLEN = 6144
WINDOW = 1536


def steps_of(own_key, extent, split, smallest, largest):
    level = 1.0
    for axis_at, blocks in split:
        heights = jax.random.uniform(jax.random.fold_in(jax.random.fold_in(own_key, 6), axis_at), (blocks,), jnp.float32, smallest / len(split), largest / len(split))
        level = level * jnp.repeat(jnp.exp(heights), extent[axis_at] // blocks).reshape((-1,) + (1,) * (len(extent) - 1 - axis_at))
    return level


def profile(amount, total, limit, skew):
    loads = [(1 << 20) // math.isqrt(standing ** skew) + 1 for standing in range(2, amount + 1)]
    rest, holding = total - limit - (amount - 1), [1] * (amount - 1)
    while rest > 0:
        movable = [i for i in range(amount - 1) if holding[i] < limit]
        pool, left = sum([loads[i] for i in movable]), rest
        for i in movable:
            extra = min(limit - holding[i], max(1, left * loads[i] // pool), rest)
            holding[i] = holding[i] + extra
            rest = rest - extra
    return np.array([limit] + holding)


def uneven(key, count, total, reach, skew):
    if count == 2:
        one = jax.random.randint(key, (), max(1, total - reach), min(reach, total - 1) + 1)
        return jnp.stack([one, total - one])
    tallies = jnp.asarray(profile(count, total, reach, skew), jnp.int32)
    couples = (count - 1) // 2
    donor, taker = tallies[1:1 + 2 * couples:2], tallies[2:2 + 2 * couples:2]
    margin = jnp.minimum(donor - 1, reach - taker)
    shifted = jax.random.randint(jax.random.fold_in(key, 1), (couples,), 0, 1 << 20) % (margin + 1)
    tallies = tallies.at[1:1 + 2 * couples:2].set(donor - shifted).at[2:2 + 2 * couples:2].set(taker + shifted)
    return tallies[jax.random.permutation(jax.random.fold_in(key, 2), count)]


def centred(key, shape, deviation, limit, split=(), held_as=jnp.bfloat16):
    result = jax.random.normal(key, shape, jnp.float32) * deviation
    if len(split) > 0:
        result = steps_of(key, shape, split, -0.22, 0.18) * result
    return jnp.clip(result, min=-limit, max=limit).astype(held_as)


def setup_inputs(seed: int = 0) -> dict:
    seeds = jax.random.split(jax.random.key(seed), 8)
    return {
        "tokens": centred(seeds[0], (TOKENS, D), 1.0, 6.0, ((0, 128),)),
        "user_ids": jnp.searchsorted(jnp.cumsum(uneven(seeds[1], USERS, TOKENS, MAXLEN, 2)), jnp.arange(TOKENS), side="right").astype(jnp.int32),
        "in_gain": jnp.clip(1.0 + 0.1 * jax.random.normal(seeds[2], (D,), jnp.float32), 0.5, 1.5),
        "out_gain": jnp.clip(1.0 + 0.1 * jax.random.normal(seeds[3], (D,), jnp.float32), 0.5, 1.5),
        "w_in": centred(seeds[4], (D, 4 * D), D ** -0.5, 0.25),
        "w_out": centred(seeds[5], (D, D), D ** -0.5, 0.25),
        "cotangent": centred(seeds[6], (TOKENS, D), 1.0, 6.0, ((0, 128),)),
    }


epsilon = 1e-05

def layer_norm(values, gain):
    center = values - lax.optimization_barrier(jnp.mean(values, axis=1, keepdims=True))
    inverse = lax.rsqrt(lax.optimization_barrier(jnp.mean(center * center, axis=1, keepdims=True)) + epsilon)
    normed = center * inverse
    return (normed * gain, normed, inverse)

def norm_backward(upstream, normed, inverse, gain):
    scaled_grad = upstream * gain
    first = lax.optimization_barrier(jnp.mean(scaled_grad, axis=1, keepdims=True))
    second = lax.optimization_barrier(jnp.mean(scaled_grad * normed, axis=1, keepdims=True))
    return (scaled_grad - first - normed * second) * inverse

def split_heads(matrix):
    return matrix.reshape(matrix.shape[0], HEADS, HEAD_DIM).astype(jnp.float32)

def pair_scores(query, keys):
    return jnp.einsum('rhd,chd->hrc', split_heads(query), split_heads(keys)) * HEAD_DIM ** (-0.5)

def pair_output(query, keys, values, key_mask):
    scores = pair_scores(query, keys)
    weights = jnp.where(key_mask[None], scores * jax.nn.sigmoid(scores), 0.0).astype(jnp.bfloat16)
    mixed = jnp.einsum('hrc,chd->rhd', weights.astype(jnp.float32), split_heads(values))
    return mixed.reshape(query.shape[0], -1)

def pair_backward(query, keys, values, key_mask, grad_attn):
    scores = pair_scores(query, keys)
    logistic = jax.nn.sigmoid(scores)
    weights = jnp.where(key_mask[None], scores * logistic, 0.0).astype(jnp.bfloat16)
    grad_weights = jnp.einsum('rhd,chd->hrc', split_heads(grad_attn), split_heads(values))
    slope = logistic * (1.0 + scores * (1.0 - logistic))
    grad_scores = (jnp.where(key_mask[None], grad_weights * slope, 0.0) * HEAD_DIM ** (-0.5)).astype(jnp.bfloat16)
    grad_scores = grad_scores.astype(jnp.float32)
    grad_query = jnp.einsum('hrc,chd->rhd', grad_scores, split_heads(keys)).reshape(query.shape[0], -1)
    grad_keys = jnp.einsum('hrc,rhd->chd', grad_scores, split_heads(query)).reshape(keys.shape[0], -1)
    grad_values = jnp.einsum('hrc,rhd->chd', weights.astype(jnp.float32), split_heads(grad_attn)).reshape(keys.shape[0], -1)
    return (grad_query, grad_keys, grad_values)

def reference(tokens, user_ids, in_gain, out_gain, w_in, w_out, cotangent):
    total_rows, model_width = tokens.shape
    blocks = total_rows // TOK_DEV
    padding = SPAN * TOK_DEV
    span_rows = (SPAN + 1) * TOK_DEV
    as_float = tokens.astype(jnp.float32)
    scaled_in, normed_in, inverse_in = layer_norm(as_float, in_gain)
    normed_tokens = scaled_in.astype(jnp.bfloat16)
    preact = jnp.dot(normed_tokens, w_in, preferred_element_type=jnp.float32)
    logistic = jax.nn.sigmoid(preact)
    projected = (preact * logistic).astype(jnp.bfloat16)
    u_part = projected[:, :model_width]
    query = projected[:, model_width:2 * model_width]
    keys = projected[:, 2 * model_width:3 * model_width]
    values = projected[:, 3 * model_width:]
    zero_rows = jnp.zeros((padding, model_width), jnp.bfloat16)
    keys_padded = jnp.concatenate([zero_rows, keys], axis=0)
    values_padded = jnp.concatenate([zero_rows, values], axis=0)
    ids_padded = jnp.concatenate([jnp.full((padding,), -1, jnp.int32), user_ids.astype(jnp.int32)], axis=0)
    positions = jnp.arange(TOK_DEV, dtype=jnp.int32)
    window_positions = jnp.arange(span_rows, dtype=jnp.int32)

    def block_inputs(block_index):
        start = (block_index * TOK_DEV).astype(jnp.int32)
        block_query = lax.dynamic_slice_in_dim(query, start, TOK_DEV, 0)
        block_ids = lax.dynamic_slice_in_dim(user_ids.astype(jnp.int32), start, TOK_DEV, 0)
        window_keys = lax.dynamic_slice_in_dim(keys_padded, start, span_rows, 0)
        window_values = lax.dynamic_slice_in_dim(values_padded, start, span_rows, 0)
        window_ids = lax.dynamic_slice_in_dim(ids_padded, start, span_rows, 0)
        key_mask = (block_ids[:, None] == window_ids[None, :]) & (window_positions[None, :] <= positions[:, None] + padding) & (window_positions[None, :] > positions[:, None] + padding - WINDOW)
        return (start, block_query, window_keys, window_values, key_mask)

    def attend(block_index):
        start, block_query, window_keys, window_values, key_mask = block_inputs(block_index)
        return pair_output(block_query, window_keys, window_values, key_mask)
    block_range = jnp.arange(blocks, dtype=jnp.int32)
    mixed = lax.map(attend, block_range).reshape(total_rows, model_width)
    scaled_out, normed_out, inverse_out = layer_norm(mixed, out_gain)
    u_float = u_part.astype(jnp.float32)
    gated = (scaled_out * u_float).astype(jnp.bfloat16)
    layer_out = (as_float + jnp.dot(gated, w_out, preferred_element_type=jnp.float32)).astype(jnp.bfloat16)
    grad_w_out = jnp.dot(gated.T, cotangent, preferred_element_type=jnp.float32)
    grad_gated = jnp.dot(cotangent, w_out.T, preferred_element_type=jnp.float32)
    grad_u = grad_gated * scaled_out
    grad_attn = norm_backward(grad_gated * u_float, normed_out, inverse_out, out_gain).astype(jnp.bfloat16)

    def backward_step(running, block_index):
        start, block_query, window_keys, window_values, key_mask = block_inputs(block_index)
        block_grad = lax.dynamic_slice_in_dim(grad_attn, start, TOK_DEV, 0)
        grad_query, grad_keys, grad_values = pair_backward(block_query, window_keys, window_values, key_mask, block_grad)
        window = lax.dynamic_slice_in_dim(running, start, span_rows, 0)
        running = lax.dynamic_update_slice_in_dim(running, window + jnp.concatenate([grad_keys, grad_values], axis=1), start, 0)
        return (running, grad_query)
    running = jnp.zeros((padding + total_rows, 2 * model_width), jnp.float32)
    running, query_grads = lax.scan(backward_step, running, block_range)
    grad_query = query_grads.reshape(total_rows, model_width)
    grad_proj = jnp.concatenate([grad_u, grad_query, running[padding:]], axis=1)
    grad_preact = (grad_proj * logistic * (1.0 + preact * (1.0 - logistic))).astype(jnp.bfloat16)
    grad_w_in = jnp.dot(normed_tokens.T, grad_preact, preferred_element_type=jnp.float32)
    grad_normed = jnp.dot(grad_preact, w_in.T, preferred_element_type=jnp.float32)
    grad_tokens = (cotangent.astype(jnp.float32) + norm_backward(grad_normed, normed_in, inverse_in, in_gain)).astype(jnp.bfloat16)
    return (layer_out, grad_tokens, grad_w_in, grad_w_out)
```

```python
import jax
import jax.numpy as jnp
from jax import lax
from jax.experimental import pallas as pl
from jax.experimental.pallas import tpu as pltpu
from jax.sharding import Mesh
from jax.sharding import PartitionSpec as P

HEADS = 4
HEAD_DIM = 128
ROWS = 768
WIDTH = 512
WINDOW_ROWS = 3 * ROWS
HALO = 2 * ROWS
TILE = 256
TILES = ROWS // TILE
SPREAD = 7
HALF_SCALE = 0.5 * HEAD_DIM ** (-0.5)
EPSILON = 1e-05
BLOCKS = 5 * HEADS
HALF_BLOCKS = BLOCKS // 2

ALL = ("z_hi", "y", "z_lo", "x", "core")
CHIPS = ("z_hi", "y", "z_lo", "x")
MIB = 1024 * 1024

f32 = jnp.float32
bf16 = jnp.bfloat16


def dot(left, right):
    return lax.dot_general(left, right, (((1,), (0,)), ((), ())), preferred_element_type=f32)


def dot_nt(left, right):
    return lax.dot_general(left, right, (((1,), (1,)), ((), ())), preferred_element_type=f32)


def layer_norm_rows(values):
    center = values - jnp.mean(values, axis=1, keepdims=True)
    inverse = lax.rsqrt(jnp.mean(center * center, axis=1, keepdims=True) + EPSILON)
    return center * inverse, inverse


def silu_and_slope(value):
    half = 0.5 * value
    tanh = jnp.tanh(half)
    silu = half + half * tanh
    slope = 0.5 * ((1.0 + tanh) + silu * (1.0 - tanh))
    return silu, slope


def project_kv(normed, w_kv, normed_t, kv, kv_t, kv_slope):
    normed_t[...] = normed.T
    for block in range(2 * HEADS):
        silu, slope = silu_and_slope(dot(normed, w_kv[:, pl.ds(block * HEAD_DIM, HEAD_DIM)]))
        silu = silu.astype(bf16)
        kv[block] = silu
        kv_t[block] = silu.T
        kv_slope[block] = slope.astype(bf16)


def own_kernel(
    tokens, in_gain, w_uq_t, w_kv, w_out, cotangent,
    normed_t, kv, kv_t, kv_slope, uq_t, uq_slope_t, grad_gated_t,
):
    normed, _ = layer_norm_rows(tokens[...].astype(f32))
    normed = (normed * in_gain[...]).astype(bf16)
    project_kv(normed, w_kv, normed_t, kv, kv_t, kv_slope)
    for block in range(2 * HEADS):
        columns = pl.ds(block * HEAD_DIM, HEAD_DIM)
        silu, slope = silu_and_slope(dot_nt(w_uq_t[columns, :], normed))
        uq_t[block] = silu.astype(bf16)
        uq_slope_t[block] = slope.astype(bf16)
    grad_gated_t[...] = dot_nt(w_out[...], cotangent[...])


def whole(shape, buffers=1):
    return pl.BlockSpec(shape, lambda *_: (0,) * len(shape), pipeline_mode=pl.Buffered(buffers))


def window_specs(at):
    blocks = 2 * HEADS
    return [
        pl.BlockSpec((WIDTH, ROWS), lambda i: (0, at(i))),
        pl.BlockSpec((blocks, ROWS, HEAD_DIM), lambda i: (0, at(i), 0)),
        pl.BlockSpec((blocks, HEAD_DIM, ROWS), lambda i: (0, 0, at(i))),
        pl.BlockSpec((blocks, ROWS, HEAD_DIM), lambda i: (0, at(i), 0)),
    ]


WINDOW_SHAPES = (
    jax.ShapeDtypeStruct((WIDTH, WINDOW_ROWS), bf16),
    jax.ShapeDtypeStruct((2 * HEADS, WINDOW_ROWS, HEAD_DIM), bf16),
    jax.ShapeDtypeStruct((2 * HEADS, HEAD_DIM, WINDOW_ROWS), bf16),
    jax.ShapeDtypeStruct((2 * HEADS, WINDOW_ROWS, HEAD_DIM), bf16),
)


def own_call(tokens, in_gain, w_uq_t, w_kv, w_out, cotangent):
    blocks = 2 * HEADS
    operands = (tokens, in_gain, w_uq_t, w_kv, w_out, cotangent)
    extra = ((blocks, HEAD_DIM, ROWS), (blocks, HEAD_DIM, ROWS), (WIDTH, ROWS))
    return pl.pallas_call(
        own_kernel,
        grid=(1,),
        in_specs=[whole(operand.shape) for operand in operands],
        out_specs=window_specs(lambda i: 2) + [whole(shape) for shape in extra],
        out_shape=WINDOW_SHAPES
        + (
            jax.ShapeDtypeStruct(extra[0], bf16),
            jax.ShapeDtypeStruct(extra[1], bf16),
            jax.ShapeDtypeStruct(extra[2], f32),
        ),
        compiler_params=pltpu.CompilerParams(vmem_limit_bytes=40 * MIB),
        cost_estimate=pl.CostEstimate(
            flops=2 * ROWS * WIDTH * 5 * WIDTH, bytes_accessed=12 * MIB, transcendentals=ROWS * 4 * WIDTH
        ),
        name="own_projection",
    )(*operands)


def halo_kernel(far, near_a, near_b, in_gain, w_kv, *refs):
    near = near_a[...].astype(f32) + near_b[...].astype(f32)
    halo = jnp.where(pl.program_id(0) == 0, far[...].astype(f32), near)
    normed, _ = layer_norm_rows(halo)
    normed = (normed * in_gain[...]).astype(bf16)
    project_kv(normed, w_kv, *refs[4:])


def halo_call(far, near_a, near_b, in_gain, w_kv, window):
    operands = (far, near_a, near_b, in_gain, w_kv)
    return pl.pallas_call(
        halo_kernel,
        grid=(2,),
        in_specs=[whole(operand.shape) for operand in operands] + [pl.BlockSpec(memory_space=pl.ANY)] * 4,
        out_specs=window_specs(lambda i: i),
        out_shape=WINDOW_SHAPES,
        input_output_aliases={5: 0, 6: 1, 7: 2, 8: 3},
        compiler_params=pltpu.CompilerParams(vmem_limit_bytes=40 * MIB),
        cost_estimate=pl.CostEstimate(
            flops=4 * ROWS * WIDTH * 2 * WIDTH, bytes_accessed=12 * MIB, transcendentals=ROWS * 4 * WIDTH
        ),
        name="halo_projection",
    )(*operands, *window)


def main_kernel(
    core, keys, values, keys_t, values_t, keys_slope, values_slope, query_t, query_slope_t,
    normed_t, u_t, u_slope_t, grad_gated_t, tokens, out_gain, w_out, cotangent, ids_row, ids_col,
    layer_out, grad_u_pre, grad_query_pre, grad_keys_pre, grad_values_pre, mine, theirs,
    mask, weights, slopes, mixed_t, grad_attn_t, grad_kv, grad_kv_pre,
):
    step_at = pl.program_id(0)
    head = lax.rem(step_at, HEADS)
    own = pl.ds(HALO, ROWS)

    def put(block, value):
        value = value.astype(bf16)
        high = jnp.where(block >= HALF_BLOCKS, 1, 0)
        at = block - high * HALF_BLOCKS

        @pl.when(core[0] == high)
        def _():
            mine[at] = value

        @pl.when(core[0] != high)
        def _():
            theirs[at] = value

    @pl.when(step_at == 0)
    def _():
        key_at = lax.broadcasted_iota(jnp.int32, (TILE, TILE), 0)
        query_at = lax.broadcasted_iota(jnp.int32, (TILE, TILE), 1)
        for tile in range(TILES):
            query_ids = ids_row[:, pl.ds(tile * TILE, TILE)]
            for step in range(SPREAD):
                allowed = ids_col[pl.ds((tile + step) * TILE, TILE), :] == query_ids
                if step == 0:
                    allowed = allowed & (key_at > query_at)
                if step == SPREAD - 1:
                    allowed = allowed & (key_at <= query_at)
                mask[tile, pl.ds(step * TILE, TILE), :] = jnp.where(allowed, 1.0, 0.0).astype(bf16)

    @pl.when(step_at < HEADS)
    def _():
        for tile in range(TILES):
            queries = pl.ds(tile * TILE, TILE)
            for step in range(SPREAD):
                at = pl.ds(step * TILE, TILE)
                scores = dot(keys[0, pl.ds((tile + step) * TILE, TILE), :], query_t[0, :, queries])
                half = scores * HALF_SCALE
                tanh = jnp.tanh(half)
                silu = half + half * tanh
                slope = (1.0 + tanh) + silu * (1.0 - tanh)
                keep = mask[tile, at, :]
                weights[head, tile, at, :] = silu.astype(bf16) * keep
                slopes[head, tile, at, :] = slope.astype(bf16) * keep
            mixed_t[head, :, queries] = dot(
                values_t[0, :, pl.ds(tile * TILE, SPREAD * TILE)], weights[head, tile]
            )

    @pl.when(step_at == HEADS)
    def _():
        gain = out_gain[...]
        for tile in range(TILES):
            rows = pl.ds(tile * TILE, TILE)
            mixed = mixed_t[:, :, rows].reshape(WIDTH, TILE)
            center = mixed - jnp.mean(mixed, axis=0, keepdims=True)
            inverse = lax.rsqrt(jnp.mean(center * center, axis=0, keepdims=True) + EPSILON)
            normed_out = center * inverse
            scaled_out = normed_out * gain
            u_part = u_t[:, :, rows].reshape(WIDTH, TILE).astype(f32)
            gated_t = (scaled_out * u_part).astype(bf16)
            upstream = grad_gated_t[:, rows]
            u_slope = u_slope_t[:, :, rows].reshape(WIDTH, TILE).astype(f32)
            grad_u_pre[:, rows] = (upstream * scaled_out * u_slope).astype(bf16)
            scaled_grad = upstream * u_part * gain
            first = jnp.mean(scaled_grad, axis=0, keepdims=True)
            second = jnp.mean(scaled_grad * normed_out, axis=0, keepdims=True)
            grad_attn = ((scaled_grad - first - normed_out * second) * inverse).astype(bf16)
            grad_attn_t[:, :, rows] = grad_attn.reshape(HEADS, HEAD_DIM, TILE)
            layer_out[rows, :] = (tokens[rows, :].astype(f32) + dot(gated_t.T, w_out[...])).astype(bf16)
            mixed_t[:, :, rows] = gated_t.astype(f32).reshape(HEADS, HEAD_DIM, TILE)
        gated_t = mixed_t[...].reshape(WIDTH, ROWS).astype(bf16)
        for block in range(HEADS):
            columns = pl.ds(block * HEAD_DIM, HEAD_DIM)
            put(4 * HEADS + block, dot(gated_t, cotangent[:, columns]))
            put(block, dot_nt(normed_t[:, own], grad_u_pre[columns, :]))

    @pl.when(step_at >= HEADS)
    def _():
        grad_kv[...] = jnp.zeros_like(grad_kv)
        for tile in range(TILES):
            queries = pl.ds(tile * TILE, TILE)
            attn_t = grad_attn_t[head, :, queries]
            for step in range(SPREAD):
                at = pl.ds(step * TILE, TILE)
                rows = pl.ds((tile + step) * TILE, TILE)
                grad_weights = dot(values[0, rows, :], attn_t)
                grad_scores = grad_weights.astype(bf16) * slopes[head, tile, at, :]
                slopes[head, tile, at, :] = grad_scores
                grad_kv[0, rows, :] += dot_nt(grad_scores, query_t[0, :, queries])
                grad_kv[1, rows, :] += dot_nt(weights[head, tile, at, :], attn_t)
            grad_query_t = dot(keys_t[0, :, pl.ds(tile * TILE, SPREAD * TILE)], slopes[head, tile])
            grad_query_pre[:, queries] = (
                grad_query_t * query_slope_t[0, :, queries].astype(f32) * HALF_SCALE
            ).astype(bf16)
        put(HEADS + head, dot_nt(normed_t[:, own], grad_query_pre[...]))
        piece = (grad_kv[0] * keys_slope[0].astype(f32) * HALF_SCALE).astype(bf16)
        grad_keys_pre[...] = piece
        grad_kv_pre[:, :HEAD_DIM] = piece
        piece = (grad_kv[1] * values_slope[0].astype(f32)).astype(bf16)
        grad_values_pre[...] = piece
        grad_kv_pre[:, HEAD_DIM:] = piece
        both = dot(normed_t[...], grad_kv_pre[...])
        put(2 * HEADS + head, both[:, :HEAD_DIM])
        put(3 * HEADS + head, both[:, HEAD_DIM:])


def main_call(core, window, uq_t, uq_slope_t, grad_gated_t, tokens, out_gain, w_out, cotangent, ids_row, ids_col):
    normed_t, kv, kv_t, kv_slope = window

    def forward_head(i):
        return lax.rem(i, HEADS)

    def backward_head(i):
        return jnp.maximum(i - HEADS, 0)

    natural, across, along = (1, WINDOW_ROWS, HEAD_DIM), (1, HEAD_DIM, WINDOW_ROWS), (1, HEAD_DIM, ROWS)
    constants = (tokens, out_gain, w_out, cotangent, ids_row, ids_col)
    in_specs = [
        pl.BlockSpec(memory_space=pltpu.SMEM),
        pl.BlockSpec(natural, lambda i: (forward_head(i), 0, 0)),
        pl.BlockSpec(natural, lambda i: (HEADS + forward_head(i), 0, 0)),
        pl.BlockSpec(across, lambda i: (forward_head(i), 0, 0)),
        pl.BlockSpec(across, lambda i: (HEADS + forward_head(i), 0, 0)),
        pl.BlockSpec(natural, lambda i: (backward_head(i), 0, 0)),
        pl.BlockSpec(natural, lambda i: (HEADS + backward_head(i), 0, 0)),
        pl.BlockSpec(along, lambda i: (HEADS + forward_head(i), 0, 0)),
        pl.BlockSpec(along, lambda i: (HEADS + backward_head(i), 0, 0)),
        whole(normed_t.shape),
        whole((HEADS, HEAD_DIM, ROWS)),
        whole((HEADS, HEAD_DIM, ROWS)),
        whole(grad_gated_t.shape),
    ] + [whole(operand.shape) for operand in constants]
    return pl.pallas_call(
        main_kernel,
        grid=(2 * HEADS,),
        in_specs=in_specs,
        out_specs=[
            whole((ROWS, WIDTH)),
            whole((WIDTH, ROWS)),
            pl.BlockSpec((HEAD_DIM, ROWS), lambda i: (backward_head(i), 0)),
            pl.BlockSpec((WINDOW_ROWS, HEAD_DIM), lambda i: (0, backward_head(i))),
            pl.BlockSpec((WINDOW_ROWS, HEAD_DIM), lambda i: (0, backward_head(i))),
            whole((HALF_BLOCKS, WIDTH, HEAD_DIM)),
            whole((HALF_BLOCKS, WIDTH, HEAD_DIM)),
        ],
        out_shape=(
            jax.ShapeDtypeStruct((ROWS, WIDTH), bf16),
            jax.ShapeDtypeStruct((WIDTH, ROWS), bf16),
            jax.ShapeDtypeStruct((WIDTH, ROWS), bf16),
            jax.ShapeDtypeStruct((WINDOW_ROWS, WIDTH), bf16),
            jax.ShapeDtypeStruct((WINDOW_ROWS, WIDTH), bf16),
            jax.ShapeDtypeStruct((HALF_BLOCKS, WIDTH, HEAD_DIM), bf16),
            jax.ShapeDtypeStruct((HALF_BLOCKS, WIDTH, HEAD_DIM), bf16),
        ),
        scratch_shapes=[
            pltpu.VMEM((TILES, SPREAD * TILE, TILE), bf16),
            pltpu.VMEM((HEADS, TILES, SPREAD * TILE, TILE), bf16),
            pltpu.VMEM((HEADS, TILES, SPREAD * TILE, TILE), bf16),
            pltpu.VMEM((HEADS, HEAD_DIM, ROWS), f32),
            pltpu.VMEM((HEADS, HEAD_DIM, ROWS), bf16),
            pltpu.VMEM((2, WINDOW_ROWS, HEAD_DIM), f32),
            pltpu.VMEM((WINDOW_ROWS, 2 * HEAD_DIM), bf16),
        ],
        compiler_params=pltpu.CompilerParams(vmem_limit_bytes=60 * MIB),
        cost_estimate=pl.CostEstimate(flops=20 * 10**9, bytes_accessed=24 * MIB, transcendentals=6 * 10**6),
        name="attention",
    )(
        core, kv, kv, kv_t, kv_t, kv_slope, kv_slope, uq_t, uq_slope_t,
        normed_t, uq_t, uq_slope_t, grad_gated_t, *constants,
    )


def back_kernel(grad_u_pre, grad_query_pre, grad_keys_pre, grad_values_pre, w_in, halo_grad, grad_normed):
    w_u, w_query, w_keys, w_values = (w_in[:, pl.ds(part * WIDTH, WIDTH)] for part in range(4))
    halo = pl.ds(0, HALO)
    own = pl.ds(HALO, ROWS)
    halo_grad[...] = (
        dot_nt(grad_keys_pre[halo, :], w_keys) + dot_nt(grad_values_pre[halo, :], w_values)
    ).astype(bf16)
    across = dot(w_u, grad_u_pre[...]) + dot(w_query, grad_query_pre[...])
    grad_normed[...] = (
        across.T + dot_nt(grad_keys_pre[own, :], w_keys) + dot_nt(grad_values_pre[own, :], w_values)
    )


def back_call(*operands):
    vmem = pl.BlockSpec(memory_space=pltpu.VMEM)
    return pl.pallas_call(
        back_kernel,
        in_specs=[vmem] * len(operands),
        out_specs=[vmem] * 2,
        out_shape=(
            jax.ShapeDtypeStruct((HALO, WIDTH), bf16),
            jax.ShapeDtypeStruct((ROWS, WIDTH), f32),
        ),
        compiler_params=pltpu.CompilerParams(vmem_limit_bytes=32 * MIB),
        cost_estimate=pl.CostEstimate(flops=32 * 10**8, bytes_accessed=14 * MIB, transcendentals=0),
        name="projection_gradient",
    )(*operands)


def unpack_kernel(core, first, second, grad_w_in, grad_w_out):
    def piece(block):
        half, at = divmod(block, HALF_BLOCKS)
        return jnp.where(core[0] == half, first[at].astype(f32), second[at].astype(f32))

    for block in range(4 * HEADS):
        grad_w_in[:, pl.ds(block * HEAD_DIM, HEAD_DIM)] = piece(block)
    for block in range(HEADS):
        grad_w_out[:, pl.ds(block * HEAD_DIM, HEAD_DIM)] = piece(4 * HEADS + block)


def unpack_call(core, first, second):
    vmem = pl.BlockSpec(memory_space=pltpu.VMEM)
    return pl.pallas_call(
        unpack_kernel,
        in_specs=[pl.BlockSpec(memory_space=pltpu.SMEM), vmem, vmem],
        out_specs=[vmem] * 2,
        out_shape=(
            jax.ShapeDtypeStruct((WIDTH, 4 * WIDTH), f32),
            jax.ShapeDtypeStruct((WIDTH, WIDTH), f32),
        ),
        compiler_params=pltpu.CompilerParams(vmem_limit_bytes=24 * MIB),
        name="unpack",
    )(core, first, second)


def step_kernel(tokens, in_gain, cotangent, grad_normed, sent, swapped, core, grad_tokens):
    normed, inverse = layer_norm_rows(tokens[...].astype(f32))
    near = jnp.where(core[0] == 0, swapped[...].astype(f32), 0.0)
    upstream = grad_normed[...] + sent[...].astype(f32) + near
    scaled_grad = upstream * in_gain[...]
    first = jnp.mean(scaled_grad, axis=1, keepdims=True)
    second = jnp.mean(scaled_grad * normed, axis=1, keepdims=True)
    grad_tokens[...] = (
        cotangent[...].astype(f32) + (scaled_grad - first - normed * second) * inverse
    ).astype(bf16)


def step_call(tokens, in_gain, cotangent, grad_normed, sent, swapped, core):
    vmem = pl.BlockSpec(memory_space=pltpu.VMEM)
    return pl.pallas_call(
        step_kernel,
        in_specs=[vmem] * 6 + [pl.BlockSpec(memory_space=pltpu.SMEM)],
        out_specs=vmem,
        out_shape=jax.ShapeDtypeStruct((ROWS, WIDTH), bf16),
        compiler_params=pltpu.CompilerParams(vmem_limit_bytes=24 * MIB),
        name="input_norm_gradient",
    )(tokens, in_gain, cotangent, grad_normed, sent, swapped, core)


def shifted(value, steps):
    count = 128
    first, last = (max(0, -steps), min(count, count - steps))
    return lax.ppermute(value, ALL, [(source, source + steps) for source in range(first, last)])


SWAP = [(0, 1), (1, 0)]


def on_device(tokens, user_ids, in_gain, out_gain, w_in, w_out, cotangent):
    core = lax.axis_index("core").astype(jnp.int32).reshape(1)
    far = shifted(tokens, 2)
    near_a = lax.ppermute(tokens, "core", [(0, 1)])
    far_ids = shifted(user_ids, 2)
    near_ids = shifted(user_ids, 1)
    near_b = lax.ppermute(far, "core", [(1, 0)])

    in_gain_row = in_gain.reshape(1, WIDTH)
    w_kv = w_in[:, 2 * WIDTH :]
    *window, uq_t, uq_slope_t, grad_gated_t = own_call(
        tokens, in_gain_row, w_in[:, : 2 * WIDTH].T, w_kv, w_out, cotangent
    )
    window = halo_call(far, near_a, near_b, in_gain_row, w_kv, window)
    window_ids = jnp.concatenate([far_ids, near_ids, user_ids])
    layer_out, *grad_pre, mine, theirs = main_call(
        core, window, uq_t, uq_slope_t, grad_gated_t, tokens, out_gain.reshape(WIDTH, 1), w_out, cotangent,
        user_ids.reshape(1, ROWS), window_ids.reshape(WINDOW_ROWS, 1),
    )
    halo_grad, grad_normed = back_call(*grad_pre, w_in)

    arrived = lax.ppermute(theirs, "core", SWAP)
    partial = (mine.astype(f32) + arrived.astype(f32)).astype(bf16).reshape(64, 80, HEAD_DIM)
    parts = lax.all_to_all(partial, CHIPS, 0, 0, tiled=True)
    total = jnp.sum(parts.astype(f32), axis=0, keepdims=True).astype(bf16)
    whole = lax.all_to_all(jnp.broadcast_to(total, (64, 80, HEAD_DIM)), CHIPS, 0, 0, tiled=True)
    whole = whole.reshape(HALF_BLOCKS, WIDTH, HEAD_DIM)
    other = lax.ppermute(whole, "core", SWAP)
    grad_w_in, grad_w_out = unpack_call(core, whole, other)

    swapped = lax.ppermute(halo_grad[ROWS:], "core", SWAP)
    outgoing = (
        halo_grad[:ROWS].astype(f32) + jnp.where(core[0] == 1, swapped.astype(f32), 0.0)
    ).astype(bf16)
    sent = shifted(outgoing, -2)
    grad_tokens = step_call(tokens, in_gain_row, cotangent, grad_normed, sent, swapped, core)
    return (layer_out, grad_tokens, grad_w_in, grad_w_out)


def solution(mesh):
    fine = Mesh(mesh.devices.reshape(2, 4, 2, 4, 2), ALL)
    placed = (P(ALL, None), P(ALL), P(), P(), P(), P(), P(ALL, None))
    return jax.shard_map(
        on_device,
        mesh=fine,
        in_specs=placed,
        out_specs=(P(ALL, None), P(ALL, None), P(), P()),
        check_vma=False,
    )
```

```python
import jax
import jax.numpy as jnp
from jax import lax
from jax.experimental import pallas as pl
from jax.experimental.pallas import tpu as pltpu
from jax.sharding import Mesh
from jax.sharding import PartitionSpec as P

HEADS = 4
HEAD_DIM = 128
ROWS = 768
WIDTH = 512
WINDOW_ROWS = 3 * ROWS
HALO = 2 * ROWS
TILE = 256
TILES = ROWS // TILE
SPREAD = 7
PAIR = 2 * HEAD_DIM
KEY_TILES = WINDOW_ROWS // TILE
HALF_SCALE = 0.5 * HEAD_DIM ** (-0.5)
EPSILON = 1e-05
BLOCKS = 5 * HEADS
HALF_BLOCKS = BLOCKS // 2

ALL = ("z_hi", "y", "z_lo", "x", "core")
CHIPS = ("z_hi", "y", "z_lo", "x")
MIB = 1024 * 1024

f32 = jnp.float32
bf16 = jnp.bfloat16


def dot(left, right):
    return lax.dot_general(left, right, (((1,), (0,)), ((), ())), preferred_element_type=f32)


def dot_nt(left, right):
    return lax.dot_general(left, right, (((1,), (1,)), ((), ())), preferred_element_type=f32)


def layer_norm_rows(values):
    center = values - jnp.mean(values, axis=1, keepdims=True)
    inverse = lax.rsqrt(jnp.mean(center * center, axis=1, keepdims=True) + EPSILON)
    return center * inverse, inverse


def silu_and_slope(value):
    half = 0.5 * value
    tanh = jnp.tanh(half)
    silu = half + half * tanh
    slope = 0.5 * ((1.0 + tanh) + silu * (1.0 - tanh))
    return silu, slope


def first_query_tile(key_tile):
    return max(0, key_tile - SPREAD + 1)


def query_tiles(key_tile):
    return range(first_query_tile(key_tile), min(TILES, key_tile + 1))


PLACE = {}
for _key_tile in range(KEY_TILES):
    for _tile in query_tiles(_key_tile):
        PLACE[_key_tile, _tile] = len(PLACE) * TILE
BAND = len(PLACE) * TILE


def project_kv(normed, w_kv, rows, normed_t, kv, kv_t, kv_slope):
    normed_t[:, rows] = normed.T
    for head in range(HEADS):
        silu, slope = silu_and_slope(dot(normed, w_kv[:, pl.ds(head * PAIR, PAIR)]))
        silu = silu.astype(bf16)
        kv_slope[head, rows, :] = slope.astype(bf16)
        for part in range(2):
            one = silu[:, part * HEAD_DIM : (part + 1) * HEAD_DIM]
            kv[part * HEADS + head, rows, :] = one
            kv_t[part * HEADS + head, :, rows] = one.T


def own_kernel(tokens, in_gain, w_uq_t, w_kv, normed_t, kv, kv_t, kv_slope, uq_t, uq_slope_t):
    for tile in range(TILES):
        rows = pl.ds(tile * TILE, TILE)
        normed, _ = layer_norm_rows(tokens[rows, :].astype(f32))
        normed = (normed * in_gain[...]).astype(bf16)
        project_kv(normed, w_kv, rows, normed_t, kv, kv_t, kv_slope)
        for block in range(2 * HEADS):
            silu, slope = silu_and_slope(dot_nt(w_uq_t[pl.ds(block * HEAD_DIM, HEAD_DIM), :], normed))
            uq_t[block, :, rows] = silu.astype(bf16)
            uq_slope_t[block, :, rows] = slope.astype(bf16)


VMEM = pl.BlockSpec(memory_space=pltpu.VMEM)
SMEM = pl.BlockSpec(memory_space=pltpu.SMEM)
ANY = pl.BlockSpec(memory_space=pl.ANY)
HBM = pl.BlockSpec(memory_space=pltpu.HBM)


def window_shapes(rows):
    return (
        (WIDTH, rows),
        (2 * HEADS, rows, HEAD_DIM),
        (2 * HEADS, HEAD_DIM, rows),
        (HEADS, rows, PAIR),
    )


def own_call(*operands):
    along = (2 * HEADS, HEAD_DIM, ROWS)
    return pl.pallas_call(
        own_kernel,
        in_specs=[VMEM] * len(operands),
        out_specs=[VMEM] * 6,
        out_shape=[jax.ShapeDtypeStruct(shape, bf16) for shape in window_shapes(ROWS) + (along, along)],
        compiler_params=pltpu.CompilerParams(vmem_limit_bytes=40 * MIB),
        cost_estimate=pl.CostEstimate(
            flops=2 * ROWS * WIDTH * 4 * WIDTH, bytes_accessed=12 * MIB, transcendentals=ROWS * 4 * WIDTH
        ),
        name="own_projection",
    )(*operands)


def relay_kernel(far, after, passed):
    del far, after, passed


def relay_call(far, after):
    return pl.pallas_call(
        relay_kernel,
        in_specs=[ANY, ANY],
        out_specs=ANY,
        out_shape=jax.ShapeDtypeStruct(far.shape, far.dtype),
        input_output_aliases={0: 0},
        name="relay",
    )(far, after)


def main_kernel(
    core, far, near_a, near_b, own_normed_t, own_kv, own_kv_t, own_kv_slope, own_uq_slope_t,
    uq_t, tokens, in_gain, out_gain, w_kv, w_out, cotangent, ids_row, ids_col,
    layer_out, grad_kv_pre, grad_uq_pre, mine, theirs,
    normed_t, kv, kv_t, kv_slope, uq_slope_t, mask, weights, slopes, mixed_t, grad_attn_t, gated_t, both, sems,
):
    own = pl.ds(HALO, ROWS)

    def staged(slot, tile):
        return weights.at[slot, :, pl.ds(tile * WIDTH, WIDTH)]

    arrivals = []
    for slot, source in enumerate((far, near_a, near_b)):
        for tile in range(TILES):
            arrivals.append(
                pltpu.make_async_copy(source.at[pl.ds(tile * TILE, TILE)], staged(slot, tile), sems.at[len(arrivals)])
            )
    fetches = [
        pltpu.make_async_copy(source, target, sems.at[len(arrivals) + at])
        for at, (source, target) in enumerate(
            (
                (own_normed_t, normed_t.at[:, own]),
                (own_kv, kv.at[:, own, :]),
                (own_kv_t, kv_t.at[:, :, own]),
                (own_kv_slope, kv_slope.at[:, own, :]),
                (own_uq_slope_t, uq_slope_t),
            )
        )
    ]
    for copy in arrivals + fetches:
        copy.start()

    key_at = lax.broadcasted_iota(jnp.int32, (TILE, TILE), 0)
    query_at = lax.broadcasted_iota(jnp.int32, (TILE, TILE), 1)
    for (key_tile, tile), place in PLACE.items():
        allowed = ids_col[pl.ds(key_tile * TILE, TILE), :] == ids_row[:, pl.ds(tile * TILE, TILE)]
        if key_tile == tile:
            allowed = allowed & (key_at > query_at)
        if key_tile == tile + SPREAD - 1:
            allowed = allowed & (key_at <= query_at)
        mask[:, pl.ds(place, TILE)] = jnp.where(allowed, 1.0, 0.0).astype(bf16)

    for copy in arrivals:
        copy.wait()
    for tile in range(2 * TILES):
        at = tile % TILES
        if tile < TILES:
            halo = staged(0, at)[...].astype(f32)
        else:
            halo = staged(1, at)[...].astype(f32) + staged(2, at)[...].astype(f32)
        normed, _ = layer_norm_rows(halo)
        normed = (normed * in_gain[...]).astype(bf16)
        project_kv(normed, w_kv, pl.ds(tile * TILE, TILE), normed_t, kv, kv_t, kv_slope)
    for copy in fetches:
        copy.wait()

    def forward(head, carry):
        for (key_tile, tile), place in PLACE.items():
            band = pl.ds(place, TILE)
            scores = dot(
                kv[head, pl.ds(key_tile * TILE, TILE), :], uq_t[HEADS + head, :, pl.ds(tile * TILE, TILE)]
            )
            half = scores * HALF_SCALE
            tanh = jnp.tanh(half)
            silu = half + half * tanh
            slope = (1.0 + tanh) + silu * (1.0 - tanh)
            keep = mask[:, band]
            weights[head, :, band] = silu.astype(bf16) * keep
            slopes[head, :, band] = slope.astype(bf16) * keep
        for tile in range(TILES):
            total = None
            for key_tile in range(tile, tile + SPREAD):
                term = dot(
                    kv_t[HEADS + head, :, pl.ds(key_tile * TILE, TILE)],
                    weights[head, :, pl.ds(PLACE[key_tile, tile], TILE)],
                )
                total = term if total is None else total + term
            mixed_t[head, :, pl.ds(tile * TILE, TILE)] = total
        return carry

    lax.fori_loop(0, HEADS, forward, 0)

    def put(block, value):
        value = value.astype(bf16)
        for part in range(2):
            at = block[part]
            high = jnp.where(at >= HALF_BLOCKS, 1, 0)
            slot = jnp.where(high == core[0], 0, 1)
            both[slot, at - high * HALF_BLOCKS] = value[:, part * HEAD_DIM : (part + 1) * HEAD_DIM]

    gain = out_gain[...]
    for tile in range(TILES):
        rows = pl.ds(tile * TILE, TILE)
        mixed = mixed_t[:, :, rows].reshape(WIDTH, TILE)
        center = mixed - jnp.mean(mixed, axis=0, keepdims=True)
        inverse = lax.rsqrt(jnp.mean(center * center, axis=0, keepdims=True) + EPSILON)
        normed_out = center * inverse
        scaled_out = normed_out * gain
        u_part = uq_t[pl.ds(0, HEADS), :, rows].reshape(WIDTH, TILE).astype(f32)
        gated = (scaled_out * u_part).astype(bf16)
        gated_t[:, rows] = gated
        upstream = dot_nt(w_out[...], cotangent[rows, :])
        u_slope = uq_slope_t[pl.ds(0, HEADS), :, rows].reshape(WIDTH, TILE).astype(f32)
        grad_u = (upstream * scaled_out * u_slope).astype(bf16)
        uq_slope_t[pl.ds(0, HEADS), :, rows] = grad_u.reshape(HEADS, HEAD_DIM, TILE)
        scaled_grad = upstream * u_part * gain
        first = jnp.mean(scaled_grad, axis=0, keepdims=True)
        second = jnp.mean(scaled_grad * normed_out, axis=0, keepdims=True)
        grad_attn = ((scaled_grad - first - normed_out * second) * inverse).astype(bf16)
        grad_attn_t[:, :, rows] = grad_attn.reshape(HEADS, HEAD_DIM, TILE)
        layer_out[rows, :] = (tokens[rows, :].astype(f32) + dot(gated.T, w_out[...])).astype(bf16)
    for pair in range(HEADS // 2):
        blocks = (2 * pair, 2 * pair + 1)
        columns = pl.ds(pair * PAIR, PAIR)
        put([4 * HEADS + block for block in blocks], dot(gated_t[...], cotangent[:, columns]))
        put(blocks, dot_nt(normed_t[:, own], uq_slope_t[pl.ds(2 * pair, 2)].reshape(PAIR, ROWS)))

    def backward(head, carry):
        for (key_tile, tile), place in PLACE.items():
            band = pl.ds(place, TILE)
            grad_weights = dot(
                kv[HEADS + head, pl.ds(key_tile * TILE, TILE), :], grad_attn_t[head, :, pl.ds(tile * TILE, TILE)]
            )
            slopes[head, :, band] = grad_weights.astype(bf16) * slopes[head, :, band]
        for key_tile in range(KEY_TILES):
            rows = pl.ds(key_tile * TILE, TILE)
            span = query_tiles(key_tile)
            band = pl.ds(PLACE[key_tile, span[0]], len(span) * TILE)
            queries = pl.ds(span[0] * TILE, len(span) * TILE)
            grad_keys = dot_nt(slopes[head, :, band], uq_t[HEADS + head, :, queries])
            grad_values = dot_nt(weights[head, :, band], grad_attn_t[head, :, queries])
            slope = kv_slope[head, rows, :].astype(f32)
            kv_slope[head, rows, :] = jnp.concatenate(
                [
                    (grad_keys * slope[:, :HEAD_DIM] * HALF_SCALE).astype(bf16),
                    (grad_values * slope[:, HEAD_DIM:]).astype(bf16),
                ],
                axis=1,
            )
        for tile in range(TILES):
            total = None
            for key_tile in range(tile, tile + SPREAD):
                term = dot(
                    kv_t[head, :, pl.ds(key_tile * TILE, TILE)],
                    slopes[head, :, pl.ds(PLACE[key_tile, tile], TILE)],
                )
                total = term if total is None else total + term
            queries = pl.ds(tile * TILE, TILE)
            slope = uq_slope_t[HEADS + head, :, queries].astype(f32)
            uq_slope_t[HEADS + head, :, queries] = (total * slope * HALF_SCALE).astype(bf16)
        put((2 * HEADS + head, 3 * HEADS + head), dot(normed_t[...], kv_slope[head]))
        return carry

    lax.fori_loop(0, HEADS, backward, 0)
    for pair in range(HEADS // 2):
        queries = uq_slope_t[pl.ds(HEADS + 2 * pair, 2)].reshape(PAIR, ROWS)
        put((HEADS + 2 * pair, HEADS + 2 * pair + 1), dot_nt(normed_t[:, own], queries))
    results = [
        pltpu.make_async_copy(source, target, sems.at[at])
        for at, (source, target) in enumerate(
            ((both.at[1], theirs), (both.at[0], mine), (kv_slope, grad_kv_pre), (uq_slope_t, grad_uq_pre))
        )
    ]
    for copy in results:
        copy.start()
    for copy in results:
        copy.wait()


def main_call(*operands):
    along = (2 * HEADS, HEAD_DIM, ROWS)
    half = (HALF_BLOCKS, WIDTH, HEAD_DIM)
    scratch = [pltpu.VMEM(shape, bf16) for shape in window_shapes(WINDOW_ROWS)] + [
        pltpu.VMEM(along, bf16),
        pltpu.VMEM((TILE, BAND), bf16),
        pltpu.VMEM((HEADS, TILE, BAND), bf16),
        pltpu.VMEM((HEADS, TILE, BAND), bf16),
        pltpu.VMEM((HEADS, HEAD_DIM, ROWS), f32),
        pltpu.VMEM((HEADS, HEAD_DIM, ROWS), bf16),
        pltpu.VMEM((WIDTH, ROWS), bf16),
        pltpu.VMEM((2,) + half, bf16),
        pltpu.SemaphoreType.DMA((16,)),
    ]
    return pl.pallas_call(
        main_kernel,
        in_specs=[SMEM] + [ANY] * 8 + [VMEM] * (len(operands) - 9),
        out_specs=[VMEM] + [ANY] * 2 + [HBM] * 2,
        out_shape=[
            jax.ShapeDtypeStruct(shape, bf16)
            for shape in ((ROWS, WIDTH), (HEADS, WINDOW_ROWS, PAIR), along, half, half)
        ],
        scratch_shapes=scratch,
        compiler_params=pltpu.CompilerParams(vmem_limit_bytes=62 * MIB),
        cost_estimate=pl.CostEstimate(flops=20 * 10**9, bytes_accessed=24 * MIB, transcendentals=6 * 10**6),
        name="attention",
    )(*operands)


def back_kernel(grad_kv_pre, grad_uq_pre, w_uq, w_kv, halo_grad, grad_normed):
    halo = pl.ds(0, HALO)
    own = pl.ds(HALO, ROWS)

    def along(rows):
        total = None
        for head in range(HEADS):
            term = dot_nt(grad_kv_pre[head, rows, :], w_kv[:, pl.ds(head * PAIR, PAIR)])
            total = term if total is None else total + term
        return total

    halo_grad[...] = along(halo).astype(bf16)
    across = dot(w_uq[...], grad_uq_pre[...].reshape(2 * WIDTH, ROWS))
    grad_normed[...] = across.T + along(own)


def back_call(*operands):
    return pl.pallas_call(
        back_kernel,
        in_specs=[VMEM] * len(operands),
        out_specs=[VMEM] * 2,
        out_shape=(
            jax.ShapeDtypeStruct((HALO, WIDTH), bf16),
            jax.ShapeDtypeStruct((ROWS, WIDTH), f32),
        ),
        compiler_params=pltpu.CompilerParams(vmem_limit_bytes=32 * MIB),
        cost_estimate=pl.CostEstimate(flops=32 * 10**8, bytes_accessed=14 * MIB, transcendentals=0),
        name="projection_gradient",
    )(*operands)


def pair_kernel(mine, arrived, total, staging, sem):
    staging[...] = (mine[...].astype(f32) + arrived[...].astype(f32)).astype(bf16)
    copy = pltpu.make_async_copy(staging, total, sem)
    copy.start()
    copy.wait()


def pair_call(mine, arrived):
    return pl.pallas_call(
        pair_kernel,
        in_specs=[VMEM] * 2,
        out_specs=HBM,
        out_shape=jax.ShapeDtypeStruct(mine.shape, bf16),
        scratch_shapes=[pltpu.VMEM(mine.shape, bf16), pltpu.SemaphoreType.DMA],
        compiler_params=pltpu.CompilerParams(vmem_limit_bytes=24 * MIB),
        name="pair_sum",
    )(mine, arrived)


def chips_kernel(parts, after, totals, staging, sem):
    del after
    total = jnp.sum(parts[...].astype(f32), axis=0, keepdims=True).astype(bf16)
    staging[...] = jnp.broadcast_to(total, staging.shape)
    copy = pltpu.make_async_copy(staging, totals, sem)
    copy.start()
    copy.wait()


def chips_call(parts, after):
    return pl.pallas_call(
        chips_kernel,
        in_specs=[VMEM, ANY],
        out_specs=HBM,
        out_shape=jax.ShapeDtypeStruct(parts.shape, bf16),
        scratch_shapes=[pltpu.VMEM(parts.shape, bf16), pltpu.SemaphoreType.DMA],
        compiler_params=pltpu.CompilerParams(vmem_limit_bytes=24 * MIB),
        name="chip_sum",
    )(parts, after)


def unpack_kernel(core, first, second, grad_w_in, grad_w_out):
    def piece(block):
        half, at = divmod(block, HALF_BLOCKS)
        return jnp.where(core[0] == half, first[at].astype(f32), second[at].astype(f32))

    for block in range(4 * HEADS):
        grad_w_in[:, pl.ds(block * HEAD_DIM, HEAD_DIM)] = piece(block)
    for block in range(HEADS):
        grad_w_out[:, pl.ds(block * HEAD_DIM, HEAD_DIM)] = piece(4 * HEADS + block)


def unpack_call(core, first, second):
    vmem = pl.BlockSpec(memory_space=pltpu.VMEM)
    return pl.pallas_call(
        unpack_kernel,
        in_specs=[pl.BlockSpec(memory_space=pltpu.SMEM), vmem, vmem],
        out_specs=[vmem] * 2,
        out_shape=(
            jax.ShapeDtypeStruct((WIDTH, 4 * WIDTH), f32),
            jax.ShapeDtypeStruct((WIDTH, WIDTH), f32),
        ),
        compiler_params=pltpu.CompilerParams(vmem_limit_bytes=24 * MIB),
        name="unpack",
    )(core, first, second)


def step_kernel(tokens, in_gain, cotangent, grad_normed, sent, swapped, core, grad_tokens):
    normed, inverse = layer_norm_rows(tokens[...].astype(f32))
    near = jnp.where(core[0] == 0, swapped[...].astype(f32), 0.0)
    upstream = grad_normed[...] + sent[...].astype(f32) + near
    scaled_grad = upstream * in_gain[...]
    first = jnp.mean(scaled_grad, axis=1, keepdims=True)
    second = jnp.mean(scaled_grad * normed, axis=1, keepdims=True)
    grad_tokens[...] = (
        cotangent[...].astype(f32) + (scaled_grad - first - normed * second) * inverse
    ).astype(bf16)


def step_call(tokens, in_gain, cotangent, grad_normed, sent, swapped, core):
    vmem = pl.BlockSpec(memory_space=pltpu.VMEM)
    return pl.pallas_call(
        step_kernel,
        in_specs=[vmem] * 6 + [pl.BlockSpec(memory_space=pltpu.SMEM)],
        out_specs=vmem,
        out_shape=jax.ShapeDtypeStruct((ROWS, WIDTH), bf16),
        compiler_params=pltpu.CompilerParams(vmem_limit_bytes=24 * MIB),
        name="input_norm_gradient",
    )(tokens, in_gain, cotangent, grad_normed, sent, swapped, core)


def shifted(value, steps):
    count = 128
    first, last = (max(0, -steps), min(count, count - steps))
    return lax.ppermute(value, ALL, [(source, source + steps) for source in range(first, last)])


SWAP = [(0, 1), (1, 0)]


def on_device(tokens, user_ids, in_gain, out_gain, w_in, w_out, cotangent):
    core = lax.axis_index("core").astype(jnp.int32).reshape(1)
    in_gain_row = in_gain.reshape(1, WIDTH)
    w_uq = w_in[:, : 2 * WIDTH]
    w_kv = w_in[:, 2 * WIDTH :].reshape(WIDTH, 2, HEADS, HEAD_DIM).transpose(0, 2, 1, 3).reshape(WIDTH, 2 * WIDTH)

    far = shifted(tokens, 2)
    near_a = lax.ppermute(tokens, "core", [(0, 1)])
    far_ids = shifted(user_ids, 2)
    near_ids = shifted(user_ids, 1)
    *window, uq_t, uq_slope_t = own_call(tokens, in_gain_row, w_uq.T, w_kv)
    far = relay_call(far, uq_t)
    near_b = lax.ppermute(far, "core", [(1, 0)])
    window_ids = jnp.concatenate([far_ids, near_ids, user_ids])
    layer_out, grad_kv_pre, grad_uq_pre, mine, theirs = main_call(
        core, far, near_a, near_b, *window, uq_slope_t,
        uq_t, tokens, in_gain_row, out_gain.reshape(WIDTH, 1), w_kv, w_out, cotangent,
        user_ids.reshape(1, ROWS), window_ids.reshape(WINDOW_ROWS, 1),
    )

    arrived = lax.ppermute(theirs, "core", SWAP)
    partial = pair_call(mine, arrived).reshape(64, 80, HEAD_DIM)
    parts = lax.all_to_all(partial, CHIPS, 0, 0, tiled=True)
    halo_grad, grad_normed = back_call(grad_kv_pre, grad_uq_pre, w_uq, w_kv)
    swapped = lax.ppermute(halo_grad[ROWS:], "core", SWAP)
    outgoing = (
        halo_grad[:ROWS].astype(f32) + jnp.where(core[0] == 1, swapped.astype(f32), 0.0)
    ).astype(bf16)
    sent = shifted(outgoing, -2)
    totals = lax.all_to_all(chips_call(parts, outgoing), CHIPS, 0, 0, tiled=True)
    totals = totals.reshape(HALF_BLOCKS, WIDTH, HEAD_DIM)
    other = lax.ppermute(totals, "core", SWAP)
    grad_tokens = step_call(tokens, in_gain_row, cotangent, grad_normed, sent, swapped, core)
    grad_w_in, grad_w_out = unpack_call(core, totals, other)
    return (layer_out, grad_tokens, grad_w_in, grad_w_out)


def solution(mesh):
    fine = Mesh(mesh.devices.reshape(2, 4, 2, 4, 2), ALL)
    placed = (P(ALL, None), P(ALL), P(), P(), P(), P(), P(ALL, None))
    return jax.shard_map(
        on_device,
        mesh=fine,
        in_specs=placed,
        out_specs=(P(ALL, None), P(ALL, None), P(), P()),
        check_vma=False,
    )
```

```python
import jax
import jax.numpy as jnp
from jax import lax
from jax.experimental import pallas as pl
from jax.experimental.pallas import tpu as pltpu
from jax.sharding import Mesh
from jax.sharding import PartitionSpec as P

HEADS = 4
HEAD_DIM = 128
ROWS = 768
WIDTH = 512
WINDOW_ROWS = 3 * ROWS
HALO = 2 * ROWS
TILE = 256
TILES = ROWS // TILE
SPREAD = 7
PAIR = 2 * HEAD_DIM
KEY_TILES = WINDOW_ROWS // TILE
HALF_SCALE = 0.5 * HEAD_DIM ** (-0.5)
EPSILON = 1e-05
BLOCKS = 5 * HEADS
HALF_BLOCKS = BLOCKS // 2

ALL = ("z_hi", "y", "z_lo", "x", "core")
CHIPS = ("z_hi", "y", "z_lo", "x")
MIB = 1024 * 1024

f32 = jnp.float32
bf16 = jnp.bfloat16


def dot(left, right):
    return lax.dot_general(left, right, (((1,), (0,)), ((), ())), preferred_element_type=f32)


def dot_nt(left, right):
    return lax.dot_general(left, right, (((1,), (1,)), ((), ())), preferred_element_type=f32)


def layer_norm_rows(values):
    center = values - jnp.mean(values, axis=1, keepdims=True)
    inverse = lax.rsqrt(jnp.mean(center * center, axis=1, keepdims=True) + EPSILON)
    return center * inverse, inverse


def silu_and_slope(value):
    half = 0.5 * value
    tanh = jnp.tanh(half)
    silu = half + half * tanh
    slope = 0.5 * ((1.0 + tanh) + silu * (1.0 - tanh))
    return silu, slope


def first_query_tile(key_tile):
    return max(0, key_tile - SPREAD + 1)


def query_tiles(key_tile):
    return range(first_query_tile(key_tile), min(TILES, key_tile + 1))


PLACE = {}
for _key_tile in range(KEY_TILES):
    for _tile in query_tiles(_key_tile):
        PLACE[_key_tile, _tile] = len(PLACE) * TILE
BAND = len(PLACE) * TILE


def project_kv(normed, w_in, rows, normed_t, kv, kv_t, kv_slope):
    normed_t[:, rows] = normed.T
    for part in range(2):
        for pair in range(HEADS // 2):
            columns = pl.ds((2 + part) * WIDTH + pair * PAIR, PAIR)
            silu, slope = silu_and_slope(dot(normed, w_in[:, columns]))
            silu = silu.astype(bf16)
            slope = slope.astype(bf16)
            for which in range(2):
                head = 2 * pair + which
                lanes = slice(which * HEAD_DIM, (which + 1) * HEAD_DIM)
                kv_slope[head, rows, pl.ds(part * HEAD_DIM, HEAD_DIM)] = slope[:, lanes]
                kv[part * HEADS + head, rows, :] = silu[:, lanes]
                kv_t[part * HEADS + head, :, rows] = silu[:, lanes].T


def own_kernel(tokens, in_gain, w_in, normed_t, kv, kv_t, kv_slope, uq_t, uq_slope_t):
    for tile in range(TILES):
        rows = pl.ds(tile * TILE, TILE)
        normed, _ = layer_norm_rows(tokens[rows, :].astype(f32))
        normed = (normed * in_gain[...]).astype(bf16)
        project_kv(normed, w_in, rows, normed_t, kv, kv_t, kv_slope)
    for pair in range(HEADS):
        w_t = w_in[:, pl.ds(pair * PAIR, PAIR)].T
        for tile in range(TILES):
            rows = pl.ds(tile * TILE, TILE)
            silu, slope = silu_and_slope(dot(w_t, normed_t[:, rows]))
            uq_t[pl.ds(2 * pair, 2), :, rows] = silu.astype(bf16).reshape(2, HEAD_DIM, TILE)
            uq_slope_t[pl.ds(2 * pair, 2), :, rows] = slope.astype(bf16).reshape(2, HEAD_DIM, TILE)


VMEM = pl.BlockSpec(memory_space=pltpu.VMEM)
SMEM = pl.BlockSpec(memory_space=pltpu.SMEM)
ANY = pl.BlockSpec(memory_space=pl.ANY)
HBM = pl.BlockSpec(memory_space=pltpu.HBM)


def window_shapes(rows):
    return (
        (WIDTH, rows),
        (2 * HEADS, rows, HEAD_DIM),
        (2 * HEADS, HEAD_DIM, rows),
        (HEADS, rows, PAIR),
    )


def own_call(*operands):
    along = (2 * HEADS, HEAD_DIM, ROWS)
    return pl.pallas_call(
        own_kernel,
        in_specs=[VMEM] * len(operands),
        out_specs=[VMEM] * 6,
        out_shape=[jax.ShapeDtypeStruct(shape, bf16) for shape in window_shapes(ROWS) + (along, along)],
        compiler_params=pltpu.CompilerParams(vmem_limit_bytes=62 * MIB),
        cost_estimate=pl.CostEstimate(
            flops=2 * ROWS * WIDTH * 4 * WIDTH, bytes_accessed=12 * MIB, transcendentals=ROWS * 4 * WIDTH
        ),
        name="own_projection",
    )(*operands)


def relay_kernel(far, after, passed):
    del far, after, passed


def relay_call(far, after):
    return pl.pallas_call(
        relay_kernel,
        in_specs=[ANY, ANY],
        out_specs=ANY,
        out_shape=jax.ShapeDtypeStruct(far.shape, far.dtype),
        input_output_aliases={0: 0},
        name="relay",
    )(far, after)


def main_kernel(
    core, far, near_a, near_b, own_normed_t, own_kv, own_kv_t, own_kv_slope, own_uq_slope_t,
    uq_t, tokens, in_gain, out_gain, w_in, w_out, cotangent, far_ids, near_ids, own_ids,
    layer_out, grad_kv_pre, grad_uq_pre, mine, theirs,
    normed_t, kv, kv_t, kv_slope, uq_slope_t, mask, weights, slopes, mixed_t, grad_attn_t, gated_t, both, sems,
):
    own = pl.ds(HALO, ROWS)

    def staged(slot, tile):
        return weights.at[slot, :, pl.ds(tile * WIDTH, WIDTH)]

    arrivals = []
    for slot, source in enumerate((far, near_a, near_b)):
        for tile in range(TILES):
            arrivals.append(
                pltpu.make_async_copy(source.at[pl.ds(tile * TILE, TILE)], staged(slot, tile), sems.at[len(arrivals)])
            )
    fetches = [
        pltpu.make_async_copy(source, target, sems.at[len(arrivals) + at])
        for at, (source, target) in enumerate(
            (
                (own_normed_t, normed_t.at[:, own]),
                (own_kv, kv.at[:, own, :]),
                (own_kv_t, kv_t.at[:, :, own]),
                (own_kv_slope, kv_slope.at[:, own, :]),
                (own_uq_slope_t, uq_slope_t),
            )
        )
    ]
    for copy in arrivals + fetches:
        copy.start()

    key_at = lax.broadcasted_iota(jnp.int32, (TILE, TILE), 0)
    query_at = lax.broadcasted_iota(jnp.int32, (TILE, TILE), 1)
    for key_tile in range(KEY_TILES):
        source = (far_ids, near_ids, own_ids)[key_tile // TILES]
        key_ids = source[:, pl.ds(key_tile % TILES * TILE, TILE)].astype(f32)
        key_ids = jnp.broadcast_to(key_ids, (TILE, TILE)).T
        for tile in query_tiles(key_tile):
            allowed = key_ids == own_ids[:, pl.ds(tile * TILE, TILE)].astype(f32)
            if key_tile == tile:
                allowed = allowed & (key_at > query_at)
            if key_tile == tile + SPREAD - 1:
                allowed = allowed & (key_at <= query_at)
            mask[:, pl.ds(PLACE[key_tile, tile], TILE)] = jnp.where(allowed, 1.0, 0.0).astype(bf16)

    for copy in arrivals:
        copy.wait()
    for tile in range(2 * TILES):
        at = tile % TILES
        if tile < TILES:
            halo = staged(0, at)[...].astype(f32)
        else:
            halo = staged(1, at)[...].astype(f32) + staged(2, at)[...].astype(f32)
        normed, _ = layer_norm_rows(halo)
        normed = (normed * in_gain[...]).astype(bf16)
        project_kv(normed, w_in, pl.ds(tile * TILE, TILE), normed_t, kv, kv_t, kv_slope)
    for copy in fetches:
        copy.wait()

    def forward(head, carry):
        for (key_tile, tile), place in PLACE.items():
            band = pl.ds(place, TILE)
            scores = dot(
                kv[head, pl.ds(key_tile * TILE, TILE), :], uq_t[HEADS + head, :, pl.ds(tile * TILE, TILE)]
            )
            half = scores * HALF_SCALE
            tanh = jnp.tanh(half)
            silu = half + half * tanh
            slope = (1.0 + tanh) + silu * (1.0 - tanh)
            keep = mask[:, band]
            weights[head, :, band] = silu.astype(bf16) * keep
            slopes[head, :, band] = slope.astype(bf16) * keep
        for tile in range(TILES):
            total = None
            for key_tile in range(tile, tile + SPREAD):
                term = dot(
                    kv_t[HEADS + head, :, pl.ds(key_tile * TILE, TILE)],
                    weights[head, :, pl.ds(PLACE[key_tile, tile], TILE)],
                )
                total = term if total is None else total + term
            mixed_t[head, :, pl.ds(tile * TILE, TILE)] = total
        return carry

    lax.fori_loop(0, HEADS, forward, 0)

    def put(block, value):
        value = value.astype(bf16)
        for part in range(2):
            at = block[part]
            high = jnp.where(at >= HALF_BLOCKS, 1, 0)
            slot = jnp.where(high == core[0], 0, 1)
            both[slot, at - high * HALF_BLOCKS] = value[:, part * HEAD_DIM : (part + 1) * HEAD_DIM]

    gain = jnp.broadcast_to(out_gain[...], (HEAD_DIM, WIDTH)).T
    gain = jnp.concatenate([gain] * (TILE // HEAD_DIM), axis=1)
    for tile in range(TILES):
        rows = pl.ds(tile * TILE, TILE)
        mixed = mixed_t[:, :, rows].reshape(WIDTH, TILE)
        center = mixed - jnp.mean(mixed, axis=0, keepdims=True)
        inverse = lax.rsqrt(jnp.mean(center * center, axis=0, keepdims=True) + EPSILON)
        normed_out = center * inverse
        scaled_out = normed_out * gain
        u_part = uq_t[pl.ds(0, HEADS), :, rows].reshape(WIDTH, TILE).astype(f32)
        gated = (scaled_out * u_part).astype(bf16)
        gated_t[:, rows] = gated
        upstream = dot_nt(w_out[...], cotangent[rows, :])
        u_slope = uq_slope_t[pl.ds(0, HEADS), :, rows].reshape(WIDTH, TILE).astype(f32)
        grad_u = (upstream * scaled_out * u_slope).astype(bf16)
        uq_slope_t[pl.ds(0, HEADS), :, rows] = grad_u.reshape(HEADS, HEAD_DIM, TILE)
        scaled_grad = upstream * u_part * gain
        first = jnp.mean(scaled_grad, axis=0, keepdims=True)
        second = jnp.mean(scaled_grad * normed_out, axis=0, keepdims=True)
        grad_attn = ((scaled_grad - first - normed_out * second) * inverse).astype(bf16)
        grad_attn_t[:, :, rows] = grad_attn.reshape(HEADS, HEAD_DIM, TILE)
        layer_out[rows, :] = (tokens[rows, :].astype(f32) + dot(gated.T, w_out[...])).astype(bf16)
    for pair in range(HEADS // 2):
        blocks = (2 * pair, 2 * pair + 1)
        columns = pl.ds(pair * PAIR, PAIR)
        put([4 * HEADS + block for block in blocks], dot(gated_t[...], cotangent[:, columns]))
        put(blocks, dot_nt(normed_t[:, own], uq_slope_t[pl.ds(2 * pair, 2)].reshape(PAIR, ROWS)))

    def backward(head, carry):
        for (key_tile, tile), place in PLACE.items():
            band = pl.ds(place, TILE)
            grad_weights = dot(
                kv[HEADS + head, pl.ds(key_tile * TILE, TILE), :], grad_attn_t[head, :, pl.ds(tile * TILE, TILE)]
            )
            slopes[head, :, band] = grad_weights.astype(bf16) * slopes[head, :, band]
        for key_tile in range(KEY_TILES):
            rows = pl.ds(key_tile * TILE, TILE)
            span = query_tiles(key_tile)
            band = pl.ds(PLACE[key_tile, span[0]], len(span) * TILE)
            queries = pl.ds(span[0] * TILE, len(span) * TILE)
            grad_keys = dot_nt(slopes[head, :, band], uq_t[HEADS + head, :, queries])
            grad_values = dot_nt(weights[head, :, band], grad_attn_t[head, :, queries])
            slope = kv_slope[head, rows, :].astype(f32)
            kv_slope[head, rows, :] = jnp.concatenate(
                [
                    (grad_keys * slope[:, :HEAD_DIM] * HALF_SCALE).astype(bf16),
                    (grad_values * slope[:, HEAD_DIM:]).astype(bf16),
                ],
                axis=1,
            )
        for tile in range(TILES):
            total = None
            for key_tile in range(tile, tile + SPREAD):
                term = dot(
                    kv_t[head, :, pl.ds(key_tile * TILE, TILE)],
                    slopes[head, :, pl.ds(PLACE[key_tile, tile], TILE)],
                )
                total = term if total is None else total + term
            queries = pl.ds(tile * TILE, TILE)
            slope = uq_slope_t[HEADS + head, :, queries].astype(f32)
            uq_slope_t[HEADS + head, :, queries] = (total * slope * HALF_SCALE).astype(bf16)
        put((2 * HEADS + head, 3 * HEADS + head), dot(normed_t[...], kv_slope[head]))
        return carry

    lax.fori_loop(0, HEADS, backward, 0)
    for pair in range(HEADS // 2):
        queries = uq_slope_t[pl.ds(HEADS + 2 * pair, 2)].reshape(PAIR, ROWS)
        put((HEADS + 2 * pair, HEADS + 2 * pair + 1), dot_nt(normed_t[:, own], queries))
    results = [
        pltpu.make_async_copy(source, target, sems.at[at])
        for at, (source, target) in enumerate(
            ((both.at[1], theirs), (both.at[0], mine), (kv_slope, grad_kv_pre), (uq_slope_t, grad_uq_pre))
        )
    ]
    for copy in results:
        copy.start()
    for copy in results:
        copy.wait()


def main_call(*operands):
    along = (2 * HEADS, HEAD_DIM, ROWS)
    half = (HALF_BLOCKS, WIDTH, HEAD_DIM)
    scratch = [pltpu.VMEM(shape, bf16) for shape in window_shapes(WINDOW_ROWS)] + [
        pltpu.VMEM(along, bf16),
        pltpu.VMEM((TILE, BAND), bf16),
        pltpu.VMEM((HEADS, TILE, BAND), bf16),
        pltpu.VMEM((HEADS, TILE, BAND), bf16),
        pltpu.VMEM((HEADS, HEAD_DIM, ROWS), f32),
        pltpu.VMEM((HEADS, HEAD_DIM, ROWS), bf16),
        pltpu.VMEM((WIDTH, ROWS), bf16),
        pltpu.VMEM((2,) + half, bf16),
        pltpu.SemaphoreType.DMA((16,)),
    ]
    return pl.pallas_call(
        main_kernel,
        in_specs=[SMEM] + [ANY] * 8 + [VMEM] * (len(operands) - 9),
        out_specs=[VMEM] + [ANY] * 2 + [HBM] * 2,
        out_shape=[
            jax.ShapeDtypeStruct(shape, bf16)
            for shape in ((ROWS, WIDTH), (HEADS, WINDOW_ROWS, PAIR), along, half, half)
        ],
        scratch_shapes=scratch,
        compiler_params=pltpu.CompilerParams(vmem_limit_bytes=62 * MIB),
        cost_estimate=pl.CostEstimate(flops=20 * 10**9, bytes_accessed=24 * MIB, transcendentals=6 * 10**6),
        name="attention",
    )(*operands)


def back_kernel(grad_kv_pre, grad_uq_pre, w_in, halo_grad, grad_normed):
    halo = pl.ds(0, HALO)
    own = pl.ds(HALO, ROWS)

    def along(rows):
        total = None
        for head in range(HEADS):
            w_pair = [w_in[:, pl.ds((2 + part) * WIDTH + head * HEAD_DIM, HEAD_DIM)] for part in range(2)]
            term = dot_nt(grad_kv_pre[head, rows, :], jnp.concatenate(w_pair, axis=1))
            total = term if total is None else total + term
        return total

    halo_grad[...] = along(halo).astype(bf16)
    across = dot(w_in[:, pl.ds(0, 2 * WIDTH)], grad_uq_pre[...].reshape(2 * WIDTH, ROWS))
    grad_normed[...] = across.T + along(own)


def back_call(*operands):
    return pl.pallas_call(
        back_kernel,
        in_specs=[VMEM] * len(operands),
        out_specs=[VMEM] * 2,
        out_shape=(
            jax.ShapeDtypeStruct((HALO, WIDTH), bf16),
            jax.ShapeDtypeStruct((ROWS, WIDTH), f32),
        ),
        compiler_params=pltpu.CompilerParams(vmem_limit_bytes=62 * MIB),
        cost_estimate=pl.CostEstimate(flops=32 * 10**8, bytes_accessed=14 * MIB, transcendentals=0),
        name="projection_gradient",
    )(*operands)


def pair_kernel(mine, arrived, total, staging, sem):
    staging[...] = (mine[...].astype(f32) + arrived[...].astype(f32)).astype(bf16)
    copy = pltpu.make_async_copy(staging, total, sem)
    copy.start()
    copy.wait()


def pair_call(mine, arrived):
    return pl.pallas_call(
        pair_kernel,
        in_specs=[VMEM] * 2,
        out_specs=HBM,
        out_shape=jax.ShapeDtypeStruct(mine.shape, bf16),
        scratch_shapes=[pltpu.VMEM(mine.shape, bf16), pltpu.SemaphoreType.DMA],
        compiler_params=pltpu.CompilerParams(vmem_limit_bytes=62 * MIB),
        name="pair_sum",
    )(mine, arrived)


def chips_kernel(parts, after, totals, staging, sem):
    del after
    total = jnp.sum(parts[...].astype(f32), axis=0, keepdims=True).astype(bf16)
    staging[...] = jnp.broadcast_to(total, staging.shape)
    copy = pltpu.make_async_copy(staging, totals, sem)
    copy.start()
    copy.wait()


def chips_call(parts, after):
    return pl.pallas_call(
        chips_kernel,
        in_specs=[VMEM, ANY],
        out_specs=HBM,
        out_shape=jax.ShapeDtypeStruct(parts.shape, bf16),
        scratch_shapes=[pltpu.VMEM(parts.shape, bf16), pltpu.SemaphoreType.DMA],
        compiler_params=pltpu.CompilerParams(vmem_limit_bytes=62 * MIB),
        name="chip_sum",
    )(parts, after)


def unpack_kernel(core, first, second, grad_w_in, grad_w_out):
    def piece(block):
        half, at = divmod(block, HALF_BLOCKS)
        return jnp.where(core[0] == half, first[at].astype(f32), second[at].astype(f32))

    for block in range(4 * HEADS):
        grad_w_in[:, pl.ds(block * HEAD_DIM, HEAD_DIM)] = piece(block)
    for block in range(HEADS):
        grad_w_out[:, pl.ds(block * HEAD_DIM, HEAD_DIM)] = piece(4 * HEADS + block)


def unpack_call(core, first, second):
    vmem = pl.BlockSpec(memory_space=pltpu.VMEM)
    return pl.pallas_call(
        unpack_kernel,
        in_specs=[pl.BlockSpec(memory_space=pltpu.SMEM), vmem, vmem],
        out_specs=[vmem] * 2,
        out_shape=(
            jax.ShapeDtypeStruct((WIDTH, 4 * WIDTH), f32),
            jax.ShapeDtypeStruct((WIDTH, WIDTH), f32),
        ),
        compiler_params=pltpu.CompilerParams(vmem_limit_bytes=62 * MIB),
        name="unpack",
    )(core, first, second)


def step_kernel(tokens, in_gain, cotangent, grad_normed, sent, swapped, core, grad_tokens):
    normed, inverse = layer_norm_rows(tokens[...].astype(f32))
    near = jnp.where(core[0] == 0, swapped[...].astype(f32), 0.0)
    upstream = grad_normed[...] + sent[...].astype(f32) + near
    scaled_grad = upstream * in_gain[...]
    first = jnp.mean(scaled_grad, axis=1, keepdims=True)
    second = jnp.mean(scaled_grad * normed, axis=1, keepdims=True)
    grad_tokens[...] = (
        cotangent[...].astype(f32) + (scaled_grad - first - normed * second) * inverse
    ).astype(bf16)


def step_call(tokens, in_gain, cotangent, grad_normed, sent, swapped, core):
    vmem = pl.BlockSpec(memory_space=pltpu.VMEM)
    return pl.pallas_call(
        step_kernel,
        in_specs=[vmem] * 6 + [pl.BlockSpec(memory_space=pltpu.SMEM)],
        out_specs=vmem,
        out_shape=jax.ShapeDtypeStruct((ROWS, WIDTH), bf16),
        compiler_params=pltpu.CompilerParams(vmem_limit_bytes=62 * MIB),
        name="input_norm_gradient",
    )(tokens, in_gain, cotangent, grad_normed, sent, swapped, core)


def shifted(value, steps):
    count = 128
    first, last = (max(0, -steps), min(count, count - steps))
    return lax.ppermute(value, ALL, [(source, source + steps) for source in range(first, last)])


SWAP = [(0, 1), (1, 0)]


def on_device(tokens, user_ids, in_gain, out_gain, w_in, w_out, cotangent):
    core = lax.axis_index("core").astype(jnp.int32).reshape(1)
    in_gain_row = in_gain.reshape(1, WIDTH)
    own_ids = user_ids.reshape(1, ROWS)

    far = shifted(tokens, 2)
    near_a = lax.ppermute(tokens, "core", [(0, 1)])
    far_ids = shifted(own_ids, 2)
    near_ids = shifted(own_ids, 1)
    *window, uq_t, uq_slope_t = own_call(tokens, in_gain_row, w_in)
    far = relay_call(far, uq_t)
    near_b = lax.ppermute(far, "core", [(1, 0)])
    layer_out, grad_kv_pre, grad_uq_pre, mine, theirs = main_call(
        core, far, near_a, near_b, *window, uq_slope_t,
        uq_t, tokens, in_gain_row, out_gain.reshape(1, WIDTH), w_in, w_out, cotangent,
        far_ids, near_ids, own_ids,
    )

    arrived = lax.ppermute(theirs, "core", SWAP)
    partial = pair_call(mine, arrived).reshape(64, 80, HEAD_DIM)
    parts = lax.all_to_all(partial, CHIPS, 0, 0, tiled=True)
    halo_grad, grad_normed = back_call(grad_kv_pre, grad_uq_pre, w_in)
    swapped = lax.ppermute(halo_grad[ROWS:], "core", SWAP)
    outgoing = (
        halo_grad[:ROWS].astype(f32) + jnp.where(core[0] == 1, swapped.astype(f32), 0.0)
    ).astype(bf16)
    sent = shifted(outgoing, -2)
    totals = lax.all_to_all(chips_call(parts, outgoing), CHIPS, 0, 0, tiled=True)
    totals = totals.reshape(HALF_BLOCKS, WIDTH, HEAD_DIM)
    other = lax.ppermute(totals, "core", SWAP)
    grad_tokens = step_call(tokens, in_gain_row, cotangent, grad_normed, sent, swapped, core)
    grad_w_in, grad_w_out = unpack_call(core, totals, other)
    return (layer_out, grad_tokens, grad_w_in, grad_w_out)


def solution(mesh):
    fine = Mesh(mesh.devices.reshape(2, 4, 2, 4, 2), ALL)
    placed = (P(ALL, None), P(ALL), P(), P(), P(), P(), P(ALL, None))
    return jax.shard_map(
        on_device,
        mesh=fine,
        in_specs=placed,
        out_specs=(P(ALL, None), P(ALL, None), P(), P()),
        check_vma=False,
    )
```

```python
import jax
import jax.numpy as jnp
from jax import lax
from jax.experimental import pallas as pl
from jax.experimental.pallas import tpu as pltpu
from jax.sharding import Mesh
from jax.sharding import PartitionSpec as P

HEADS = 4
HEAD_DIM = 128
ROWS = 768
WIDTH = 512
WINDOW_ROWS = 3 * ROWS
HALO = 2 * ROWS
TILE = 256
TILES = ROWS // TILE
SPREAD = 7
PAIR = 2 * HEAD_DIM
KEY_TILES = WINDOW_ROWS // TILE
HALF_SCALE = 0.5 * HEAD_DIM ** (-0.5)
EPSILON = 1e-05
BLOCKS = 5 * HEADS
HALF_BLOCKS = BLOCKS // 2

ALL = ("z_hi", "y", "z_lo", "x", "core")
CHIPS = ("z_hi", "y", "z_lo", "x")
MIB = 1024 * 1024

f32 = jnp.float32
bf16 = jnp.bfloat16


def dot(left, right):
    return lax.dot_general(left, right, (((1,), (0,)), ((), ())), preferred_element_type=f32)


def dot_nt(left, right):
    return lax.dot_general(left, right, (((1,), (1,)), ((), ())), preferred_element_type=f32)


def layer_norm_rows(values):
    center = values - jnp.mean(values, axis=1, keepdims=True)
    inverse = lax.rsqrt(jnp.mean(center * center, axis=1, keepdims=True) + EPSILON)
    return center * inverse, inverse


def silu_and_slope(value):
    half = 0.5 * value
    tanh = jnp.tanh(half)
    silu = half + half * tanh
    slope = 0.5 * ((1.0 + tanh) + silu * (1.0 - tanh))
    return silu, slope


def first_query_tile(key_tile):
    return max(0, key_tile - SPREAD + 1)


def query_tiles(key_tile):
    return range(first_query_tile(key_tile), min(TILES, key_tile + 1))


PLACE = {}
for _key_tile in range(KEY_TILES):
    for _tile in query_tiles(_key_tile):
        PLACE[_key_tile, _tile] = len(PLACE) * TILE
BAND = len(PLACE) * TILE


def project_kv(normed, w_in, rows, normed_t, kv, kv_t, kv_slope):
    normed_t[:, rows] = normed.T
    for part in range(2):
        for pair in range(HEADS // 2):
            columns = pl.ds((2 + part) * WIDTH + pair * PAIR, PAIR)
            silu, slope = silu_and_slope(dot(normed, w_in[:, columns]))
            silu = silu.astype(bf16)
            kv_slope[part, rows, pl.ds(pair * PAIR, PAIR)] = slope.astype(bf16)
            for which in range(2):
                head = 2 * pair + which
                lanes = slice(which * HEAD_DIM, (which + 1) * HEAD_DIM)
                kv[part * HEADS + head, rows, :] = silu[:, lanes]
                kv_t[part * HEADS + head, :, rows] = silu[:, lanes].T


def own_kernel(tokens, in_gain, w_in, normed_t, kv, kv_t, kv_slope, uq_t, uq_slope_t):
    for tile in range(TILES):
        rows = pl.ds(tile * TILE, TILE)
        normed, _ = layer_norm_rows(tokens[rows, :].astype(f32))
        normed = (normed * in_gain[...]).astype(bf16)
        project_kv(normed, w_in, rows, normed_t, kv, kv_t, kv_slope)
    for pair in range(HEADS):
        w_t = w_in[:, pl.ds(pair * PAIR, PAIR)].T
        for tile in range(TILES):
            rows = pl.ds(tile * TILE, TILE)
            silu, slope = silu_and_slope(dot(w_t, normed_t[:, rows]))
            uq_t[pl.ds(2 * pair, 2), :, rows] = silu.astype(bf16).reshape(2, HEAD_DIM, TILE)
            uq_slope_t[pl.ds(2 * pair, 2), :, rows] = slope.astype(bf16).reshape(2, HEAD_DIM, TILE)


VMEM = pl.BlockSpec(memory_space=pltpu.VMEM)
SMEM = pl.BlockSpec(memory_space=pltpu.SMEM)
ANY = pl.BlockSpec(memory_space=pl.ANY)
HBM = pl.BlockSpec(memory_space=pltpu.HBM)


def window_shapes(rows):
    return (
        (WIDTH, rows),
        (2 * HEADS, rows, HEAD_DIM),
        (2 * HEADS, HEAD_DIM, rows),
        (2, rows, WIDTH),
    )


def own_call(*operands):
    along = (2 * HEADS, HEAD_DIM, ROWS)
    return pl.pallas_call(
        own_kernel,
        in_specs=[VMEM] * len(operands),
        out_specs=[VMEM] * 6,
        out_shape=[jax.ShapeDtypeStruct(shape, bf16) for shape in window_shapes(ROWS) + (along, along)],
        compiler_params=pltpu.CompilerParams(vmem_limit_bytes=62 * MIB),
        cost_estimate=pl.CostEstimate(
            flops=2 * ROWS * WIDTH * 4 * WIDTH, bytes_accessed=12 * MIB, transcendentals=ROWS * 4 * WIDTH
        ),
        name="own_projection",
    )(*operands)


def relay_kernel(*refs):
    del refs


def slow_relay_call(far, *after):
    return pl.pallas_call(
        relay_kernel,
        in_specs=[ANY] * (1 + len(after)),
        out_specs=ANY,
        out_shape=jax.ShapeDtypeStruct(far.shape, far.dtype),
        input_output_aliases={0: 0},
        cost_estimate=pl.CostEstimate(flops=10*10**9, bytes_accessed=0, transcendentals=0),
        name='relay_home',
    )(far, *after)


def relay_call(far, *after):
    return pl.pallas_call(
        relay_kernel,
        in_specs=[ANY] * (1 + len(after)),
        out_specs=ANY,
        out_shape=jax.ShapeDtypeStruct(far.shape, far.dtype),
        input_output_aliases={0: 0},
        name="relay",
    )(far, *after)


def main_kernel(
    core, far, near_a, near_b, own_normed_t, own_kv, own_kv_t, own_kv_slope, own_uq_slope_t,
    uq_t, tokens, in_gain, out_gain, w_in, w_out, cotangent, far_ids, near_ids, own_ids,
    layer_out, grad_kv_pre, grad_uq_pre, far_grad, near_grad, mine, theirs,
    normed_t, kv, kv_t, kv_slope, uq_slope_t, mask, weights, slopes, mixed_t, grad_attn_t, gated_t, both, sems,
):
    own = pl.ds(HALO, ROWS)

    def staged(slot, tile):
        return weights.at[slot, :, pl.ds(tile * WIDTH, WIDTH)]

    arrivals = []
    for slot, source in enumerate((far, near_a, near_b)):
        for tile in range(TILES):
            arrivals.append(
                pltpu.make_async_copy(source.at[pl.ds(tile * TILE, TILE)], staged(slot, tile), sems.at[len(arrivals)])
            )
    fetches = [
        pltpu.make_async_copy(source, target, sems.at[len(arrivals) + at])
        for at, (source, target) in enumerate(
            (
                (own_normed_t, normed_t.at[:, own]),
                (own_kv, kv.at[:, own, :]),
                (own_kv_t, kv_t.at[:, :, own]),
                (own_kv_slope, kv_slope.at[:, own, :]),
                (own_uq_slope_t, uq_slope_t),
            )
        )
    ]
    for copy in arrivals + fetches:
        copy.start()

    key_at = lax.broadcasted_iota(jnp.int32, (TILE, TILE), 0)
    query_at = lax.broadcasted_iota(jnp.int32, (TILE, TILE), 1)
    for key_tile in range(KEY_TILES):
        source = (far_ids, near_ids, own_ids)[key_tile // TILES]
        key_ids = source[:, pl.ds(key_tile % TILES * TILE, TILE)].astype(f32)
        key_ids = jnp.broadcast_to(key_ids, (TILE, TILE)).T
        for tile in query_tiles(key_tile):
            allowed = key_ids == own_ids[:, pl.ds(tile * TILE, TILE)].astype(f32)
            if key_tile == tile:
                allowed = allowed & (key_at > query_at)
            if key_tile == tile + SPREAD - 1:
                allowed = allowed & (key_at <= query_at)
            mask[:, pl.ds(PLACE[key_tile, tile], TILE)] = jnp.where(allowed, 1.0, 0.0).astype(bf16)

    for copy in arrivals:
        copy.wait()
    for tile in range(2 * TILES):
        at = tile % TILES
        if tile < TILES:
            halo = staged(0, at)[...].astype(f32)
        else:
            halo = staged(1, at)[...].astype(f32) + staged(2, at)[...].astype(f32)
        normed, _ = layer_norm_rows(halo)
        normed = (normed * in_gain[...]).astype(bf16)
        project_kv(normed, w_in, pl.ds(tile * TILE, TILE), normed_t, kv, kv_t, kv_slope)
    for copy in fetches:
        copy.wait()

    def forward(head, carry):
        for (key_tile, tile), place in PLACE.items():
            band = pl.ds(place, TILE)
            scores = dot(
                kv[head, pl.ds(key_tile * TILE, TILE), :], uq_t[HEADS + head, :, pl.ds(tile * TILE, TILE)]
            )
            half = scores * HALF_SCALE
            tanh = jnp.tanh(half)
            silu = half + half * tanh
            slope = (1.0 + tanh) + silu * (1.0 - tanh)
            keep = mask[:, band]
            weights[head, :, band] = silu.astype(bf16) * keep
            slopes[head, :, band] = slope.astype(bf16) * keep
        for tile in range(TILES):
            total = None
            for key_tile in range(tile, tile + SPREAD):
                term = dot(
                    kv_t[HEADS + head, :, pl.ds(key_tile * TILE, TILE)],
                    weights[head, :, pl.ds(PLACE[key_tile, tile], TILE)],
                )
                total = term if total is None else total + term
            mixed_t[head, :, pl.ds(tile * TILE, TILE)] = total
        return carry

    lax.fori_loop(0, HEADS, forward, 0)

    def put(block, value):
        value = value.astype(bf16)
        for part in range(2):
            at = block[part]
            high = jnp.where(at >= HALF_BLOCKS, 1, 0)
            slot = jnp.where(high == core[0], 0, 1)
            both[slot, at - high * HALF_BLOCKS] = value[:, part * HEAD_DIM : (part + 1) * HEAD_DIM]

    gain = jnp.broadcast_to(out_gain[...], (HEAD_DIM, WIDTH)).T
    gain = jnp.concatenate([gain] * (TILE // HEAD_DIM), axis=1)
    for tile in range(TILES):
        rows = pl.ds(tile * TILE, TILE)
        mixed = mixed_t[:, :, rows].reshape(WIDTH, TILE)
        center = mixed - jnp.mean(mixed, axis=0, keepdims=True)
        inverse = lax.rsqrt(jnp.mean(center * center, axis=0, keepdims=True) + EPSILON)
        normed_out = center * inverse
        scaled_out = normed_out * gain
        u_part = uq_t[pl.ds(0, HEADS), :, rows].reshape(WIDTH, TILE).astype(f32)
        gated = (scaled_out * u_part).astype(bf16)
        gated_t[:, rows] = gated
        upstream = dot_nt(w_out[...], cotangent[rows, :])
        u_slope = uq_slope_t[pl.ds(0, HEADS), :, rows].reshape(WIDTH, TILE).astype(f32)
        grad_u = (upstream * scaled_out * u_slope).astype(bf16)
        uq_slope_t[pl.ds(0, HEADS), :, rows] = grad_u.reshape(HEADS, HEAD_DIM, TILE)
        scaled_grad = upstream * u_part * gain
        first = jnp.mean(scaled_grad, axis=0, keepdims=True)
        second = jnp.mean(scaled_grad * normed_out, axis=0, keepdims=True)
        grad_attn = ((scaled_grad - first - normed_out * second) * inverse).astype(bf16)
        grad_attn_t[:, :, rows] = grad_attn.reshape(HEADS, HEAD_DIM, TILE)
        layer_out[rows, :] = (tokens[rows, :].astype(f32) + dot(gated.T, w_out[...])).astype(bf16)
    for pair in range(HEADS // 2):
        blocks = (2 * pair, 2 * pair + 1)
        columns = pl.ds(pair * PAIR, PAIR)
        put([4 * HEADS + block for block in blocks], dot(gated_t[...], cotangent[:, columns]))
        put(blocks, dot_nt(normed_t[:, own], uq_slope_t[pl.ds(2 * pair, 2)].reshape(PAIR, ROWS)))

    def backward(head, carry):
        columns = pl.ds(pl.multiple_of(head * HEAD_DIM, HEAD_DIM), HEAD_DIM)
        for (key_tile, tile), place in PLACE.items():
            band = pl.ds(place, TILE)
            grad_weights = dot(
                kv[HEADS + head, pl.ds(key_tile * TILE, TILE), :], grad_attn_t[head, :, pl.ds(tile * TILE, TILE)]
            )
            slopes[head, :, band] = grad_weights.astype(bf16) * slopes[head, :, band]
        for key_tile in range(KEY_TILES):
            rows = pl.ds(key_tile * TILE, TILE)
            span = query_tiles(key_tile)
            band = pl.ds(PLACE[key_tile, span[0]], len(span) * TILE)
            queries = pl.ds(span[0] * TILE, len(span) * TILE)
            grad_keys = dot_nt(slopes[head, :, band], uq_t[HEADS + head, :, queries])
            grad_values = dot_nt(weights[head, :, band], grad_attn_t[head, :, queries])
            slope = kv_slope[0, rows, columns].astype(f32)
            kv_slope[0, rows, columns] = (grad_keys * slope * HALF_SCALE).astype(bf16)
            slope = kv_slope[1, rows, columns].astype(f32)
            kv_slope[1, rows, columns] = (grad_values * slope).astype(bf16)
        for tile in range(TILES):
            total = None
            for key_tile in range(tile, tile + SPREAD):
                term = dot(
                    kv_t[head, :, pl.ds(key_tile * TILE, TILE)],
                    slopes[head, :, pl.ds(PLACE[key_tile, tile], TILE)],
                )
                total = term if total is None else total + term
            queries = pl.ds(tile * TILE, TILE)
            slope = uq_slope_t[HEADS + head, :, queries].astype(f32)
            uq_slope_t[HEADS + head, :, queries] = (total * slope * HALF_SCALE).astype(bf16)
        return carry

    lax.fori_loop(0, HEADS, backward, 0)

    departures = []
    for tile in range(2 * TILES):
        rows = pl.ds(tile * TILE, TILE)
        total = sum(
            dot_nt(kv_slope[part, rows, :], w_in[:, pl.ds((2 + part) * WIDTH, WIDTH)]) for part in range(2)
        )
        slot, at = divmod(tile, TILES)
        staged(slot, at)[...] = total.astype(bf16)
        target = (far_grad, near_grad)[slot].at[pl.ds(at * TILE, TILE)]
        departures.append(pltpu.make_async_copy(staged(slot, at), target, sems.at[tile]))
        departures[-1].start()
    results = [
        pltpu.make_async_copy(source, target, sems.at[len(departures) + at])
        for at, (source, target) in enumerate(
            (
                (kv_slope.at[:, own, :], grad_kv_pre),
                (uq_slope_t, grad_uq_pre),
                (both.at[1], theirs),
                (both.at[0], mine),
            )
        )
    ]
    results[0].start()
    results[1].start()
    for pair in range(HEADS // 2):
        blocks = (2 * pair, 2 * pair + 1)
        queries = uq_slope_t[pl.ds(HEADS + 2 * pair, 2)].reshape(PAIR, ROWS)
        put([HEADS + block for block in blocks], dot_nt(normed_t[:, own], queries))
        for part in range(2):
            columns = pl.ds(pair * PAIR, PAIR)
            put([(2 + part) * HEADS + block for block in blocks], dot(normed_t[...], kv_slope[part, :, columns]))
    results[2].start()
    results[3].start()
    for copy in departures + results:
        copy.wait()


def main_call(*operands):
    along = (2 * HEADS, HEAD_DIM, ROWS)
    half = (HALF_BLOCKS, WIDTH, HEAD_DIM)
    scratch = [pltpu.VMEM(shape, bf16) for shape in window_shapes(WINDOW_ROWS)] + [
        pltpu.VMEM(along, bf16),
        pltpu.VMEM((TILE, BAND), bf16),
        pltpu.VMEM((HEADS, TILE, BAND), bf16),
        pltpu.VMEM((HEADS, TILE, BAND), bf16),
        pltpu.VMEM((HEADS, HEAD_DIM, ROWS), f32),
        pltpu.VMEM((HEADS, HEAD_DIM, ROWS), bf16),
        pltpu.VMEM((WIDTH, ROWS), bf16),
        pltpu.VMEM((2,) + half, bf16),
        pltpu.SemaphoreType.DMA((16,)),
    ]
    return pl.pallas_call(
        main_kernel,
        in_specs=[SMEM] + [ANY] * 8 + [VMEM] * (len(operands) - 9),
        out_specs=[VMEM] + [ANY] * 6,
        out_shape=[
            jax.ShapeDtypeStruct(shape, bf16)
            for shape in ((ROWS, WIDTH), (2, ROWS, WIDTH), along, (ROWS, WIDTH), (ROWS, WIDTH), half, half)
        ],
        scratch_shapes=scratch,
        compiler_params=pltpu.CompilerParams(vmem_limit_bytes=62 * MIB),
        cost_estimate=pl.CostEstimate(flops=20 * 10**9, bytes_accessed=24 * MIB, transcendentals=6 * 10**6),
        name="attention",
    )(*operands)


def back_kernel(grad_kv_pre, grad_uq_pre, w_in, after, grad_normed):
    del after
    across = dot(w_in[:, pl.ds(0, 2 * WIDTH)], grad_uq_pre[...].reshape(2 * WIDTH, ROWS))
    along = sum(dot_nt(grad_kv_pre[part], w_in[:, pl.ds((2 + part) * WIDTH, WIDTH)]) for part in range(2))
    grad_normed[...] = across.T + along


def back_call(*operands):
    return pl.pallas_call(
        back_kernel,
        in_specs=[VMEM] * 3 + [ANY],
        out_specs=VMEM,
        out_shape=jax.ShapeDtypeStruct((ROWS, WIDTH), f32),
        compiler_params=pltpu.CompilerParams(vmem_limit_bytes=24 * MIB),
        cost_estimate=pl.CostEstimate(flops=16 * 10**8, bytes_accessed=8 * MIB, transcendentals=0),
        name="projection_gradient",
    )(*operands)


def pair_kernel(core, mine, arrived, far_grad, swapped, total, outgoing):
    total[...] = (mine[...].astype(f32) + arrived[...].astype(f32)).astype(bf16)
    near = jnp.where(core[0] == 1, swapped[...].astype(f32), 0.0)
    outgoing[...] = (far_grad[...].astype(f32) + near).astype(bf16)


def pair_call(core, mine, arrived, far_grad, swapped):
    return pl.pallas_call(
        pair_kernel,
        in_specs=[SMEM] + [VMEM] * 4,
        out_specs=[VMEM] * 2,
        out_shape=[jax.ShapeDtypeStruct(like.shape, bf16) for like in (mine, far_grad)],
        compiler_params=pltpu.CompilerParams(vmem_limit_bytes=24 * MIB),
        name="pair_sum",
    )(core, mine, arrived, far_grad, swapped)


def chips_kernel(parts, after, totals, staging, sem):
    del after
    total = jnp.sum(parts[...].astype(f32), axis=0, keepdims=True).astype(bf16)
    staging[...] = jnp.broadcast_to(total, staging.shape)
    copy = pltpu.make_async_copy(staging, totals, sem)
    copy.start()
    copy.wait()


def chips_call(parts, after):
    return pl.pallas_call(
        chips_kernel,
        in_specs=[VMEM, ANY],
        out_specs=HBM,
        out_shape=jax.ShapeDtypeStruct(parts.shape, bf16),
        scratch_shapes=[pltpu.VMEM(parts.shape, bf16), pltpu.SemaphoreType.DMA],
        compiler_params=pltpu.CompilerParams(vmem_limit_bytes=62 * MIB),
        name="chip_sum",
    )(parts, after)


def unpack_kernel(core, first, second, grad_w_in, grad_w_out):
    def piece(block):
        half, at = divmod(block, HALF_BLOCKS)
        return jnp.where(core[0] == half, first[at].astype(f32), second[at].astype(f32))

    for block in range(4 * HEADS):
        grad_w_in[:, pl.ds(block * HEAD_DIM, HEAD_DIM)] = piece(block)
    for block in range(HEADS):
        grad_w_out[:, pl.ds(block * HEAD_DIM, HEAD_DIM)] = piece(4 * HEADS + block)


def unpack_call(core, first, second):
    vmem = pl.BlockSpec(memory_space=pltpu.VMEM)
    return pl.pallas_call(
        unpack_kernel,
        in_specs=[pl.BlockSpec(memory_space=pltpu.SMEM), vmem, vmem],
        out_specs=[vmem] * 2,
        out_shape=(
            jax.ShapeDtypeStruct((WIDTH, 4 * WIDTH), f32),
            jax.ShapeDtypeStruct((WIDTH, WIDTH), f32),
        ),
        compiler_params=pltpu.CompilerParams(vmem_limit_bytes=24 * MIB),
        name="unpack",
    )(core, first, second)


def step_kernel(tokens, in_gain, cotangent, grad_normed, sent, swapped, core, grad_tokens):
    normed, inverse = layer_norm_rows(tokens[...].astype(f32))
    near = jnp.where(core[0] == 0, swapped[...].astype(f32), 0.0)
    upstream = grad_normed[...] + sent[...].astype(f32) + near
    scaled_grad = upstream * in_gain[...]
    first = jnp.mean(scaled_grad, axis=1, keepdims=True)
    second = jnp.mean(scaled_grad * normed, axis=1, keepdims=True)
    grad_tokens[...] = (
        cotangent[...].astype(f32) + (scaled_grad - first - normed * second) * inverse
    ).astype(bf16)


def step_call(*operands):
    return pl.pallas_call(
        step_kernel,
        in_specs=[VMEM] * 6 + [SMEM],
        out_specs=VMEM,
        out_shape=jax.ShapeDtypeStruct((ROWS, WIDTH), bf16),
        compiler_params=pltpu.CompilerParams(vmem_limit_bytes=24 * MIB),
        name="input_norm_gradient",
    )(*operands)


def shifted(value, steps):
    count = 128
    first, last = (max(0, -steps), min(count, count - steps))
    return lax.ppermute(value, ALL, [(source, source + steps) for source in range(first, last)])


SWAP = [(0, 1), (1, 0)]


def on_device(tokens, user_ids, in_gain, out_gain, w_in, w_out, cotangent):
    core = lax.axis_index("core").astype(jnp.int32).reshape(1)
    in_gain_row = in_gain.reshape(1, WIDTH)
    own_ids = user_ids.reshape(1, ROWS)

    far = shifted(tokens, 2)
    near_a = lax.ppermute(tokens, "core", [(0, 1)])
    far_ids = shifted(own_ids, 2)
    near_ids = shifted(own_ids, 1)
    *window, uq_t, uq_slope_t = own_call(tokens, in_gain_row, w_in)
    far = relay_call(far, uq_t, far_ids, near_ids)
    near_b = lax.ppermute(far, "core", [(1, 0)])
    layer_out, grad_kv_pre, grad_uq_pre, far_grad, near_grad, mine, theirs = main_call(
        core, far, near_a, near_b, *window, uq_slope_t,
        uq_t, tokens, in_gain_row, out_gain.reshape(1, WIDTH), w_in, w_out, cotangent,
        far_ids, near_ids, own_ids,
    )

    arrived = lax.ppermute(theirs, "core", SWAP)
    swapped = lax.ppermute(near_grad, "core", SWAP)
    partial, outgoing = pair_call(core, mine, arrived, far_grad, swapped)
    sent = slow_relay_call(shifted(outgoing, -2))
    grad_normed = back_call(grad_kv_pre, grad_uq_pre, w_in, outgoing)
    parts = lax.all_to_all(partial.reshape(64, 80, HEAD_DIM), CHIPS, 0, 0, tiled=True)
    total = chips_call(parts, grad_normed)
    totals = lax.all_to_all(total, CHIPS, 0, 0, tiled=True)
    grad_tokens = step_call(tokens, in_gain_row, cotangent, grad_normed, sent, swapped, core)
    totals = relay_call(totals.reshape(HALF_BLOCKS, WIDTH, HEAD_DIM), grad_tokens)
    other = lax.ppermute(totals, "core", SWAP)
    grad_w_in, grad_w_out = unpack_call(core, totals, other)
    return (layer_out, grad_tokens, grad_w_in, grad_w_out)


def solution(mesh):
    fine = Mesh(mesh.devices.reshape(2, 4, 2, 4, 2), ALL)
    placed = (P(ALL, None), P(ALL), P(), P(), P(), P(), P(ALL, None))
    return jax.shard_map(
        on_device,
        mesh=fine,
        in_specs=placed,
        out_specs=(P(ALL, None), P(ALL, None), P(), P()),
        check_vma=False,
    )
```

```python
import functools

import jax
import jax.numpy as jnp
from jax import lax
from jax.experimental import pallas as pl
from jax.experimental.pallas import tpu as pltpu
from jax.sharding import Mesh
from jax.sharding import PartitionSpec as P

HEADS = 4
HEAD_DIM = 128
ROWS = 768
WIDTH = 512
WINDOW_ROWS = 3 * ROWS
HALO = 2 * ROWS
TILE = 256
TILES = ROWS // TILE
SPREAD = 7
PAIR = 2 * HEAD_DIM
KEY_TILES = WINDOW_ROWS // TILE
HALF_SCALE = 0.5 * HEAD_DIM ** (-0.5)
EPSILON = 1e-05
BLOCKS = 5 * HEADS
HALF_BLOCKS = BLOCKS // 2

ALL = ("z_hi", "y", "z_lo", "x", "core")
CHIPS = ("z_hi", "y", "z_lo", "x")
MIB = 1024 * 1024

f32 = jnp.float32
bf16 = jnp.bfloat16


def dot(left, right):
    return lax.dot_general(left, right, (((1,), (0,)), ((), ())), preferred_element_type=f32)


def dot_nt(left, right):
    return lax.dot_general(left, right, (((1,), (1,)), ((), ())), preferred_element_type=f32)


def layer_norm_rows(values):
    center = values - jnp.mean(values, axis=1, keepdims=True)
    inverse = lax.rsqrt(jnp.mean(center * center, axis=1, keepdims=True) + EPSILON)
    return center * inverse, inverse


def silu_and_slope(value):
    half = 0.5 * value
    tanh = jnp.tanh(half)
    silu = (half + half * tanh).astype(bf16)
    tanh = tanh.astype(bf16)
    slope = 0.5 * ((1.0 + tanh) + silu * (1.0 - tanh))
    return silu, slope


def first_query_tile(key_tile):
    return max(0, key_tile - SPREAD + 1)


def query_tiles(key_tile):
    return range(first_query_tile(key_tile), min(TILES, key_tile + 1))


PLACE = {}
for _key_tile in range(KEY_TILES):
    for _tile in query_tiles(_key_tile):
        PLACE[_key_tile, _tile] = len(PLACE) * TILE
BAND = len(PLACE) * TILE


def project_kv(normed, w_kv, rows, normed_t, kv, kv_t, kv_slope):
    normed_t[:, rows] = normed.T
    for part in range(2):
        for pair in range(HEADS // 2):
            columns = pl.ds(part * WIDTH + pair * PAIR, PAIR)
            silu, slope = silu_and_slope(dot(normed, w_kv[:, columns]))
            kv_slope[part, rows, pl.ds(pair * PAIR, PAIR)] = slope
            for which in range(2):
                head = 2 * pair + which
                lanes = slice(which * HEAD_DIM, (which + 1) * HEAD_DIM)
                kv[part * HEADS + head, rows, :] = silu[:, lanes]
                kv_t[part * HEADS + head, :, rows] = silu[:, lanes].T


def own_kernel(
    tokens, in_gain, w_in, out_normed_t, out_kv, out_kv_t, out_kv_slope, out_uq_t, out_uq_slope_t,
    normed_t, kv, kv_t, kv_slope, uq_t, uq_slope_t, w_uq, w_kv, sems,
):
    fetches = [
        pltpu.make_async_copy(w_in.at[:, pl.ds(part * 2 * WIDTH, 2 * WIDTH)], target, sems.at[part])
        for part, target in enumerate((w_uq, w_kv))
    ]
    fetches[1].start()
    fetches[0].start()
    fetches[1].wait()
    for tile in range(TILES):
        rows = pl.ds(tile * TILE, TILE)
        normed, _ = layer_norm_rows(tokens[rows, :].astype(f32))
        normed = (normed * in_gain[...]).astype(bf16)
        project_kv(normed, w_kv, rows, normed_t, kv, kv_t, kv_slope)
    results = [
        pltpu.make_async_copy(source, target, sems.at[2 + at])
        for at, (source, target) in enumerate(
            ((kv, out_kv), (kv_t, out_kv_t), (kv_slope, out_kv_slope), (normed_t, out_normed_t))
        )
    ]
    for copy in results:
        copy.start()
    fetches[0].wait()
    for pair in range(HEADS):
        w_t = w_uq[:, pl.ds(pair * PAIR, PAIR)].T
        both = pl.ds(2 * pair, 2)
        for tile in range(TILES):
            rows = pl.ds(tile * TILE, TILE)
            silu, slope = silu_and_slope(dot(w_t, normed_t[:, rows]))
            uq_t[both, :, rows] = silu.reshape(2, HEAD_DIM, TILE)
            uq_slope_t[both, :, rows] = slope.reshape(2, HEAD_DIM, TILE)
        for source, target in ((uq_t, out_uq_t), (uq_slope_t, out_uq_slope_t)):
            results.append(pltpu.make_async_copy(source.at[both], target.at[both], sems.at[2 + len(results)]))
            results[-1].start()
    for copy in results:
        copy.wait()


VMEM = pl.BlockSpec(memory_space=pltpu.VMEM)
SMEM = pl.BlockSpec(memory_space=pltpu.SMEM)
ANY = pl.BlockSpec(memory_space=pl.ANY)
HBM = pl.BlockSpec(memory_space=pltpu.HBM)


def window_shapes(rows):
    return (
        (WIDTH, rows),
        (2 * HEADS, rows, HEAD_DIM),
        (2 * HEADS, HEAD_DIM, rows),
        (2, rows, WIDTH),
    )


def own_call(*operands):
    along = (2 * HEADS, HEAD_DIM, ROWS)
    shapes = window_shapes(ROWS) + (along, along)
    return pl.pallas_call(
        own_kernel,
        in_specs=[VMEM, VMEM, ANY],
        out_specs=[ANY] * 6,
        out_shape=[jax.ShapeDtypeStruct(shape, bf16) for shape in shapes],
        scratch_shapes=[pltpu.VMEM(shape, bf16) for shape in shapes + ((WIDTH, 2 * WIDTH),) * 2]
        + [pltpu.SemaphoreType.DMA((14,))],
        compiler_params=pltpu.CompilerParams(vmem_limit_bytes=62 * MIB),
        cost_estimate=pl.CostEstimate(
            flops=2 * ROWS * WIDTH * 4 * WIDTH, bytes_accessed=12 * MIB, transcendentals=ROWS * 4 * WIDTH
        ),
        name="own_projection",
    )(*operands)


def relay_kernel(*refs):
    del refs


def slow_relay_call(far, *after):
    return pl.pallas_call(
        relay_kernel,
        in_specs=[ANY] * (1 + len(after)),
        out_specs=ANY,
        out_shape=jax.ShapeDtypeStruct(far.shape, far.dtype),
        input_output_aliases={0: 0},
        cost_estimate=pl.CostEstimate(flops=10*10**9, bytes_accessed=0, transcendentals=0),
        name='relay_home',
    )(far, *after)


def relay_call(far, *after):
    return pl.pallas_call(
        relay_kernel,
        in_specs=[ANY] * (1 + len(after)),
        out_specs=ANY,
        out_shape=jax.ShapeDtypeStruct(far.shape, far.dtype),
        input_output_aliases={0: 0},
        name="relay",
    )(far, *after)


def main_kernel(
    core, in_gain, out_gain, far_ids, near_ids, own_ids,
    far, near_a, near_b, w_in, own_kv, own_uq_t, own_kv_t, own_uq_slope_t, own_w_out, own_cotangent, own_tokens,
    own_normed_t, own_kv_slope,
    out_rows, grad_kv_pre, grad_uq_pre, far_grad, near_grad, mine, theirs,
    normed_t, kv, kv_t, kv_slope, uq_t, uq_slope_t, mask, weights, slopes, mixed_t, grad_attn_t, gated_t, both,
    w_kv, w_out, cotangent, tokens, layer_out, sems,
):
    own = pl.ds(HALO, ROWS)

    def staged(slot, tile):
        return weights.at[slot, :, pl.ds(tile * WIDTH, WIDTH)]

    def starter(source, target):
        copy = pltpu.make_async_copy(source, target, sems.at[len(copies)])
        copies.append(copy)
        copy.start()
        return copy

    copies = []
    starter(w_in.at[:, pl.ds(2 * WIDTH, 2 * WIDTH)], w_kv)
    for slot, source in enumerate((far, near_a, near_b)):
        for tile in range(TILES):
            starter(source.at[pl.ds(tile * TILE, TILE)], staged(slot, tile))
    arrivals = list(copies)
    starter(own_kv, kv.at[:, own, :])
    starter(own_uq_t, uq_t)
    starter(own_kv_t, kv_t.at[:, :, own])
    for_forward = copies[len(arrivals) :]
    starter(own_uq_slope_t, uq_slope_t)
    starter(own_w_out, w_out)
    starter(own_cotangent, cotangent)
    starter(own_tokens, tokens)
    starter(own_normed_t, normed_t.at[:, own])
    starter(own_kv_slope, kv_slope.at[:, own, :])
    for_backward = copies[len(arrivals) + len(for_forward) :]

    key_at = lax.broadcasted_iota(jnp.int32, (TILE, TILE), 0)
    query_at = lax.broadcasted_iota(jnp.int32, (TILE, TILE), 1)
    for key_tile in range(KEY_TILES):
        source = (far_ids, near_ids, own_ids)[key_tile // TILES]
        key_ids = source[:, pl.ds(key_tile % TILES * TILE, TILE)].astype(f32)
        key_ids = jnp.broadcast_to(key_ids, (TILE, TILE)).T
        for tile in query_tiles(key_tile):
            allowed = key_ids == own_ids[:, pl.ds(tile * TILE, TILE)].astype(f32)
            if key_tile == tile:
                allowed = allowed & (key_at > query_at)
            if key_tile == tile + SPREAD - 1:
                allowed = allowed & (key_at <= query_at)
            mask[:, pl.ds(PLACE[key_tile, tile], TILE)] = jnp.where(allowed, 1.0, 0.0).astype(bf16)

    for copy in arrivals:
        copy.wait()
    for tile in range(2 * TILES):
        at = tile % TILES
        if tile < TILES:
            halo = staged(0, at)[...].astype(f32)
        else:
            halo = staged(1, at)[...].astype(f32) + staged(2, at)[...].astype(f32)
        normed, _ = layer_norm_rows(halo)
        normed = (normed * in_gain[...]).astype(bf16)
        project_kv(normed, w_kv, pl.ds(tile * TILE, TILE), normed_t, kv, kv_t, kv_slope)
    for copy in for_forward:
        copy.wait()

    def forward(head, carry):
        for (key_tile, tile), place in PLACE.items():
            band = pl.ds(place, TILE)
            scores = dot(
                kv[head, pl.ds(key_tile * TILE, TILE), :], uq_t[HEADS + head, :, pl.ds(tile * TILE, TILE)]
            )
            half = (scores * HALF_SCALE).astype(bf16)
            tanh = jnp.tanh(half)
            silu = half + half * tanh
            slope = (1.0 + tanh) + silu * (1.0 - tanh)
            keep = mask[:, band]
            weights[head, :, band] = silu * keep
            slopes[head, :, band] = slope * keep
        for tile in range(TILES):
            total = None
            for key_tile in range(tile, tile + SPREAD):
                term = dot(
                    kv_t[HEADS + head, :, pl.ds(key_tile * TILE, TILE)],
                    weights[head, :, pl.ds(PLACE[key_tile, tile], TILE)],
                )
                total = term if total is None else total + term
            mixed_t[head, :, pl.ds(tile * TILE, TILE)] = total
        return carry

    lax.fori_loop(0, HEADS, forward, 0)

    def put(block, value):
        value = value.astype(bf16)
        for part in range(2):
            at = block[part]
            high = jnp.where(at >= HALF_BLOCKS, 1, 0)
            slot = jnp.where(high == core[0], 0, 1)
            both[slot, at - high * HALF_BLOCKS] = value[:, part * HEAD_DIM : (part + 1) * HEAD_DIM]

    for copy in for_backward:
        copy.wait()
    gain = jnp.broadcast_to(out_gain[...], (HEAD_DIM, WIDTH)).T
    gain = jnp.concatenate([gain] * (TILE // HEAD_DIM), axis=1)
    for tile in range(TILES):
        rows = pl.ds(tile * TILE, TILE)
        mixed = mixed_t[:, :, rows].reshape(WIDTH, TILE)
        center = mixed - jnp.mean(mixed, axis=0, keepdims=True)
        inverse = lax.rsqrt(jnp.mean(center * center, axis=0, keepdims=True) + EPSILON)
        normed_out = center * inverse
        scaled_out = normed_out * gain
        u_part = uq_t[pl.ds(0, HEADS), :, rows].reshape(WIDTH, TILE).astype(f32)
        gated = (scaled_out * u_part).astype(bf16)
        gated_t[:, rows] = gated
        upstream = dot_nt(w_out[...], cotangent[rows, :])
        u_slope = uq_slope_t[pl.ds(0, HEADS), :, rows].reshape(WIDTH, TILE).astype(f32)
        grad_u = (upstream * scaled_out * u_slope).astype(bf16)
        uq_slope_t[pl.ds(0, HEADS), :, rows] = grad_u.reshape(HEADS, HEAD_DIM, TILE)
        scaled_grad = upstream * u_part * gain
        first = jnp.mean(scaled_grad, axis=0, keepdims=True)
        second = jnp.mean(scaled_grad * normed_out, axis=0, keepdims=True)
        grad_attn = ((scaled_grad - first - normed_out * second) * inverse).astype(bf16)
        grad_attn_t[:, :, rows] = grad_attn.reshape(HEADS, HEAD_DIM, TILE)
        layer_out[rows, :] = (tokens[rows, :].astype(f32) + dot(gated.T, w_out[...])).astype(bf16)
    for pair in range(HEADS // 2):
        blocks = (2 * pair, 2 * pair + 1)
        columns = pl.ds(pair * PAIR, PAIR)
        put([4 * HEADS + block for block in blocks], dot(gated_t[...], cotangent[:, columns]))
        put(blocks, dot_nt(normed_t[:, own], uq_slope_t[pl.ds(2 * pair, 2)].reshape(PAIR, ROWS)))

    departures = [pltpu.make_async_copy(layer_out, out_rows, sems.at[0])]
    departures[0].start()

    def backward(head, carry):
        columns = pl.ds(pl.multiple_of(head * HEAD_DIM, HEAD_DIM), HEAD_DIM)
        for (key_tile, tile), place in PLACE.items():
            band = pl.ds(place, TILE)
            grad_weights = dot(
                kv[HEADS + head, pl.ds(key_tile * TILE, TILE), :], grad_attn_t[head, :, pl.ds(tile * TILE, TILE)]
            )
            slopes[head, :, band] = grad_weights.astype(bf16) * slopes[head, :, band]
        for key_tile in range(KEY_TILES):
            rows = pl.ds(key_tile * TILE, TILE)
            span = query_tiles(key_tile)
            band = pl.ds(PLACE[key_tile, span[0]], len(span) * TILE)
            queries = pl.ds(span[0] * TILE, len(span) * TILE)
            grad_keys = dot_nt(slopes[head, :, band], uq_t[HEADS + head, :, queries])
            grad_values = dot_nt(weights[head, :, band], grad_attn_t[head, :, queries])
            slope = kv_slope[0, rows, columns].astype(f32)
            kv_slope[0, rows, columns] = (grad_keys * slope * HALF_SCALE).astype(bf16)
            slope = kv_slope[1, rows, columns].astype(f32)
            kv_slope[1, rows, columns] = (grad_values * slope).astype(bf16)
        for tile in range(TILES):
            total = None
            for key_tile in range(tile, tile + SPREAD):
                term = dot(
                    kv_t[head, :, pl.ds(key_tile * TILE, TILE)],
                    slopes[head, :, pl.ds(PLACE[key_tile, tile], TILE)],
                )
                total = term if total is None else total + term
            queries = pl.ds(tile * TILE, TILE)
            slope = uq_slope_t[HEADS + head, :, queries].astype(f32)
            uq_slope_t[HEADS + head, :, queries] = (total * slope * HALF_SCALE).astype(bf16)
        return carry

    lax.fori_loop(0, HEADS, backward, 0)

    def depart(source, target):
        departures.append(pltpu.make_async_copy(source, target, sems.at[len(departures)]))
        departures[-1].start()

    def half_done(half):
        at = len(departures)
        departures.append(pltpu.make_async_copy(both.at[0], mine, sems.at[at]))

        @pl.when(core[0] == half)
        def _():
            pltpu.make_async_copy(both.at[0], mine, sems.at[at]).start()

        @pl.when(core[0] != half)
        def _():
            pltpu.make_async_copy(both.at[1], theirs, sems.at[at]).start()

    def put_pair(part, pair):
        blocks = [part * HEADS + 2 * pair + which for which in range(2)]
        columns = pl.ds(pair * PAIR, PAIR)
        if part == 1:
            queries = uq_slope_t[pl.ds(HEADS + 2 * pair, 2)].reshape(PAIR, ROWS)
            put(blocks, dot_nt(normed_t[:, own], queries))
        else:
            put(blocks, dot(normed_t[...], kv_slope[part - 2, :, columns]))

    for tile in range(2 * TILES):
        rows = pl.ds(tile * TILE, TILE)
        total = sum(dot_nt(kv_slope[part, rows, :], w_kv[:, pl.ds(part * WIDTH, WIDTH)]) for part in range(2))
        slot, at = divmod(tile, TILES)
        staged(slot, at)[...] = total.astype(bf16)
        depart(staged(slot, at), (far_grad, near_grad)[slot].at[pl.ds(at * TILE, TILE)])
    depart(kv_slope.at[:, own, :], grad_kv_pre)
    depart(uq_slope_t, grad_uq_pre)
    for part, pair in ((1, 0), (1, 1), (2, 0)):
        put_pair(part, pair)
    half_done(0)
    for part, pair in ((2, 1), (3, 0), (3, 1)):
        put_pair(part, pair)
    half_done(1)
    for copy in departures:
        copy.wait()


def main_call(*operands):
    along = (2 * HEADS, HEAD_DIM, ROWS)
    half = (HALF_BLOCKS, WIDTH, HEAD_DIM)
    scratch = [pltpu.VMEM(shape, bf16) for shape in window_shapes(WINDOW_ROWS)] + [
        pltpu.VMEM(along, bf16),
        pltpu.VMEM(along, bf16),
        pltpu.VMEM((TILE, BAND), bf16),
        pltpu.VMEM((HEADS, TILE, BAND), bf16),
        pltpu.VMEM((HEADS, TILE, BAND), bf16),
        pltpu.VMEM((HEADS, HEAD_DIM, ROWS), f32),
        pltpu.VMEM((HEADS, HEAD_DIM, ROWS), bf16),
        pltpu.VMEM((WIDTH, ROWS), bf16),
        pltpu.VMEM((2,) + half, bf16),
        pltpu.VMEM((WIDTH, 2 * WIDTH), bf16),
        pltpu.VMEM((WIDTH, WIDTH), bf16),
        pltpu.VMEM((ROWS, WIDTH), bf16),
        pltpu.VMEM((ROWS, WIDTH), bf16),
        pltpu.VMEM((ROWS, WIDTH), bf16),
        pltpu.SemaphoreType.DMA((20,)),
    ]
    return pl.pallas_call(
        main_kernel,
        in_specs=[SMEM] + [VMEM] * 5 + [ANY] * (len(operands) - 6),
        out_specs=[ANY] * 7,
        out_shape=[
            jax.ShapeDtypeStruct(shape, bf16)
            for shape in ((ROWS, WIDTH), (2, ROWS, WIDTH), along, (ROWS, WIDTH), (ROWS, WIDTH), half, half)
        ],
        scratch_shapes=scratch,
        compiler_params=pltpu.CompilerParams(vmem_limit_bytes=62 * MIB),
        cost_estimate=pl.CostEstimate(flops=20 * 10**9, bytes_accessed=24 * MIB, transcendentals=6 * 10**6),
        name="attention",
    )(*operands)


def back_kernel(grad_kv_pre, grad_uq_pre, w_in, after, grad_normed):
    del after
    across = dot(w_in[:, pl.ds(0, 2 * WIDTH)], grad_uq_pre[...].reshape(2 * WIDTH, ROWS))
    along = sum(dot_nt(grad_kv_pre[part], w_in[:, pl.ds((2 + part) * WIDTH, WIDTH)]) for part in range(2))
    grad_normed[...] = across.T + along


def back_call(*operands):
    return pl.pallas_call(
        back_kernel,
        in_specs=[VMEM] * 3 + [ANY],
        out_specs=VMEM,
        out_shape=jax.ShapeDtypeStruct((ROWS, WIDTH), f32),
        compiler_params=pltpu.CompilerParams(vmem_limit_bytes=24 * MIB),
        cost_estimate=pl.CostEstimate(flops=16 * 10**8, bytes_accessed=8 * MIB, transcendentals=0),
        name="projection_gradient",
    )(*operands)


PIECES = 4


def pair_kernel(core, mine, arrived, far_grad, swapped, total, out_a, out_b, held, others, homes, nears, sems, out_sems):
    rows = HALF_BLOCKS * WIDTH // PIECES
    home_rows = ROWS // 2
    copies = []

    def start(source, target):
        copies.append(pltpu.make_async_copy(source, target, sems.at[len(copies)]))
        copies[-1].start()

    for half in range(2):
        at = pl.ds(half * home_rows, home_rows)
        start(far_grad.at[at], homes.at[at])
        start(swapped.at[at], nears.at[at])
    for piece in range(PIECES):
        at = pl.ds(piece * rows, rows)
        start(mine.at[at], held.at[at])
        start(arrived.at[at], others.at[at])
    results = []

    def finish(source, target):
        results.append(pltpu.make_async_copy(source, target, out_sems.at[len(results)]))
        results[-1].start()

    for half, target in enumerate((out_a, out_b)):
        at = pl.ds(half * home_rows, home_rows)
        copies[2 * half].wait()
        copies[2 * half + 1].wait()
        near = jnp.where(core[0] == 1, nears[at, :].astype(f32), 0.0)
        homes[at, :] = (homes[at, :].astype(f32) + near).astype(bf16)
        finish(homes.at[at], target)
    for piece in range(PIECES):
        at = pl.ds(piece * rows, rows)
        copies[4 + 2 * piece].wait()
        copies[5 + 2 * piece].wait()
        held[at, :] = (held[at, :].astype(f32) + others[at, :].astype(f32)).astype(bf16)
        finish(held.at[at], total.at[at])
    for copy in results:
        copy.wait()


def pair_call(core, *operands):
    half = (HALF_BLOCKS * WIDTH, HEAD_DIM)
    home = (ROWS, WIDTH)
    return pl.pallas_call(
        pair_kernel,
        in_specs=[SMEM] + [ANY] * 4,
        out_specs=[ANY] * 3,
        out_shape=[jax.ShapeDtypeStruct(shape, bf16) for shape in (half, (ROWS // 2, WIDTH), (ROWS // 2, WIDTH))],
        scratch_shapes=[pltpu.VMEM(shape, bf16) for shape in (half, half, home, home)]
        + [pltpu.SemaphoreType.DMA((4 + 2 * PIECES,)), pltpu.SemaphoreType.DMA((2 + PIECES,))],
        compiler_params=pltpu.CompilerParams(vmem_limit_bytes=62 * MIB),
        name="pair_sum",
    )(core, *operands)


def chips_kernel(parts, *refs):
    totals = refs[-1]
    total = jnp.sum(parts[...].astype(f32), axis=0, keepdims=True).astype(bf16)
    totals[...] = jnp.broadcast_to(total, totals.shape)


def chips_call(parts, *after):
    return pl.pallas_call(
        chips_kernel,
        in_specs=[VMEM] + [ANY] * len(after),
        out_specs=VMEM,
        out_shape=jax.ShapeDtypeStruct(parts.shape, bf16),
        compiler_params=pltpu.CompilerParams(vmem_limit_bytes=24 * MIB),
        name="chip_sum",
    )(parts, *after)


def unpack_kernel(flip, core, blocks, *refs):
    grad_w_in, grad_w_out, staging, sems = refs[-4:]
    for half in range(2):

        @pl.when(core[0] == half ^ flip)
        def _(half=half):
            copies = []
            for at in range(HALF_BLOCKS):
                staging[at] = blocks[at].astype(f32)
                block = half * HALF_BLOCKS + at
                if block < 4 * HEADS:
                    target = grad_w_in.at[:, pl.ds(block * HEAD_DIM, HEAD_DIM)]
                else:
                    target = grad_w_out.at[:, pl.ds((block - 4 * HEADS) * HEAD_DIM, HEAD_DIM)]
                copies.append(pltpu.make_async_copy(staging.at[at], target, sems.at[at]))
                copies[-1].start()
            for copy in copies:
                copy.wait()


def unpack_call(core, blocks, flip, into=()):
    return pl.pallas_call(
        functools.partial(unpack_kernel, flip),
        in_specs=[SMEM, VMEM] + [ANY] * len(into),
        out_specs=[ANY] * 2,
        out_shape=(
            jax.ShapeDtypeStruct((WIDTH, 4 * WIDTH), f32),
            jax.ShapeDtypeStruct((WIDTH, WIDTH), f32),
        ),
        scratch_shapes=[
            pltpu.VMEM((HALF_BLOCKS, WIDTH, HEAD_DIM), f32),
            pltpu.SemaphoreType.DMA((HALF_BLOCKS,)),
        ],
        input_output_aliases={2: 0, 3: 1} if into else {},
        compiler_params=pltpu.CompilerParams(vmem_limit_bytes=24 * MIB),
        name="unpack",
    )(core, blocks, *into)


def step_kernel(
    core, in_gain, tokens, cotangent, grad_normed, sent_a, sent_b, swapped, after, grad_tokens,
    rows_in, cot, grad, sent, near, result, sems, out_sems,
):
    del after
    half = ROWS // 2
    copies = []
    for part, sent_half in enumerate((sent_a, sent_b)):
        at = pl.ds(part * half, half)
        for source, target in (
            (tokens.at[at], rows_in.at[at]),
            (grad_normed.at[at], grad.at[at]),
            (swapped.at[at], near.at[at]),
            (sent_half, sent.at[at]),
            (cotangent.at[at], cot.at[at]),
        ):
            copies.append(pltpu.make_async_copy(source, target, sems.at[len(copies)]))
            copies[-1].start()
    results = []
    for part in range(2):
        at = pl.ds(part * half, half)
        copies[5 * part].wait()
        normed, inverse = layer_norm_rows(rows_in[at, :].astype(f32))
        for copy in copies[5 * part + 1 : 5 * part + 5]:
            copy.wait()
        home = jnp.where(core[0] == 0, near[at, :].astype(f32), 0.0)
        scaled_grad = (grad[at, :] + sent[at, :].astype(f32) + home) * in_gain[...]
        first = jnp.mean(scaled_grad, axis=1, keepdims=True)
        second = jnp.mean(scaled_grad * normed, axis=1, keepdims=True)
        result[at, :] = (
            cot[at, :].astype(f32) + (scaled_grad - first - normed * second) * inverse
        ).astype(bf16)
        results.append(pltpu.make_async_copy(result.at[at], grad_tokens.at[at], out_sems.at[part]))
        results[-1].start()
    for copy in results:
        copy.wait()


def step_call(*operands):
    shape = (ROWS, WIDTH)
    return pl.pallas_call(
        step_kernel,
        in_specs=[SMEM, VMEM] + [ANY] * 7,
        out_specs=ANY,
        out_shape=jax.ShapeDtypeStruct(shape, bf16),
        scratch_shapes=[pltpu.VMEM(shape, kind) for kind in (bf16, bf16, f32, bf16, bf16, bf16)]
        + [pltpu.SemaphoreType.DMA((10,)), pltpu.SemaphoreType.DMA((2,))],
        compiler_params=pltpu.CompilerParams(vmem_limit_bytes=62 * MIB),
        name="input_norm_gradient",
    )(*operands)


def shifted(value, steps):
    count = 128
    first, last = (max(0, -steps), min(count, count - steps))
    return lax.ppermute(value, ALL, [(source, source + steps) for source in range(first, last)])


SWAP = [(0, 1), (1, 0)]


def on_device(tokens, user_ids, in_gain, out_gain, w_in, w_out, cotangent):
    core = lax.axis_index("core").astype(jnp.int32).reshape(1)
    in_gain_row = in_gain.reshape(1, WIDTH)
    own_ids = user_ids.reshape(1, ROWS)

    far = shifted(tokens, 2)
    near_a = lax.ppermute(tokens, "core", [(0, 1)])
    far_ids = shifted(own_ids, 2)
    near_ids = shifted(own_ids, 1)
    *window, uq_t, uq_slope_t = own_call(tokens, in_gain_row, w_in)
    far = relay_call(far, uq_t, far_ids, near_ids)
    near_b = lax.ppermute(far, "core", [(1, 0)])
    normed_t, kv, kv_t, kv_slope = window
    layer_out, grad_kv_pre, grad_uq_pre, far_grad, near_grad, mine, theirs = main_call(
        core, in_gain_row, out_gain.reshape(1, WIDTH), far_ids, near_ids, own_ids,
        far, near_a, near_b, w_in, kv, uq_t, kv_t, uq_slope_t, w_out, cotangent, tokens, normed_t, kv_slope,
    )

    arrived = lax.ppermute(theirs, "core", SWAP)
    swapped = lax.ppermute(near_grad, "core", SWAP)
    flat = (HALF_BLOCKS * WIDTH, HEAD_DIM)
    partial, out_a, out_b = pair_call(core, mine.reshape(flat), arrived.reshape(flat), far_grad, swapped)
    sent_a = slow_relay_call(shifted(out_a, -2))
    sent_b = slow_relay_call(shifted(out_b, -2))
    grad_normed = back_call(grad_kv_pre, grad_uq_pre, w_in, out_b)
    parts = lax.all_to_all(partial.reshape(64, 80, HEAD_DIM), CHIPS, 0, 0, tiled=True)
    totals = lax.all_to_all(chips_call(parts, grad_normed, sent_a), CHIPS, 0, 0, tiled=True)
    totals = totals.reshape(HALF_BLOCKS, WIDTH, HEAD_DIM)
    other = lax.ppermute(totals, "core", SWAP)
    halves = unpack_call(core, totals, 0)
    grad_w_in, grad_w_out = unpack_call(core, other, 1, halves)
    grad_tokens = step_call(
        core, in_gain_row, tokens, cotangent, grad_normed, sent_a, sent_b, swapped, grad_w_out,
    )
    return (layer_out, grad_tokens, grad_w_in, grad_w_out)


def solution(mesh):
    fine = Mesh(mesh.devices.reshape(2, 4, 2, 4, 2), ALL)
    placed = (P(ALL, None), P(ALL), P(), P(), P(), P(), P(ALL, None))
    return jax.shard_map(
        on_device,
        mesh=fine,
        in_specs=placed,
        out_specs=(P(ALL, None), P(ALL, None), P(), P()),
        check_vma=False,
    )
```

```python
import functools

import jax
import jax.numpy as jnp
from jax import lax
from jax.experimental import pallas as pl
from jax.experimental.pallas import tpu as pltpu
from jax.sharding import Mesh
from jax.sharding import PartitionSpec as P

HEADS = 4
HEAD_DIM = 128
ROWS = 768
WIDTH = 512
WINDOW_ROWS = 3 * ROWS
HALO = 2 * ROWS
TILE = 256
TILES = ROWS // TILE
SPREAD = 7
PAIR = 2 * HEAD_DIM
KEY_TILES = WINDOW_ROWS // TILE
HALF_SCALE = 0.5 * HEAD_DIM ** (-0.5)
EPSILON = 1e-05
BLOCKS = 5 * HEADS
HALF_BLOCKS = BLOCKS // 2

ALL = ("z_hi", "y", "z_lo", "x", "core")
CHIPS = ("z_hi", "y", "z_lo", "x")
MIB = 1024 * 1024

f32 = jnp.float32
bf16 = jnp.bfloat16


def dot(left, right):
    return lax.dot_general(left, right, (((1,), (0,)), ((), ())), preferred_element_type=f32)


def dot_nt(left, right):
    return lax.dot_general(left, right, (((1,), (1,)), ((), ())), preferred_element_type=f32)


def layer_norm_rows(values):
    center = values - jnp.mean(values, axis=1, keepdims=True)
    inverse = lax.rsqrt(jnp.mean(center * center, axis=1, keepdims=True) + EPSILON)
    return center * inverse, inverse


def silu_and_slope(value):
    half = 0.5 * value
    tanh = jnp.tanh(half)
    silu = (half + half * tanh).astype(bf16)
    tanh = tanh.astype(bf16)
    slope = 0.5 * ((1.0 + tanh) + silu * (1.0 - tanh))
    return silu, slope


def first_query_tile(key_tile):
    return max(0, key_tile - SPREAD + 1)


def query_tiles(key_tile):
    return range(first_query_tile(key_tile), min(TILES, key_tile + 1))


PLACE = {}
for _key_tile in range(KEY_TILES):
    for _tile in query_tiles(_key_tile):
        PLACE[_key_tile, _tile] = len(PLACE) * TILE
BAND = len(PLACE) * TILE


def project_kv(normed, w_kv, rows, normed_t, kv, kv_t, kv_slope):
    normed_t[:, rows] = normed.T
    for part in range(2):
        for pair in range(HEADS // 2):
            columns = pl.ds(part * WIDTH + pair * PAIR, PAIR)
            silu, slope = silu_and_slope(dot(normed, w_kv[:, columns]))
            kv_slope[part, rows, pl.ds(pair * PAIR, PAIR)] = slope
            for which in range(2):
                head = 2 * pair + which
                lanes = slice(which * HEAD_DIM, (which + 1) * HEAD_DIM)
                kv[part * HEADS + head, rows, :] = silu[:, lanes]
                kv_t[part * HEADS + head, :, rows] = silu[:, lanes].T


def own_kernel(
    tokens, in_gain, w_in, out_normed_t, out_kv, out_kv_t, out_kv_slope, out_uq_t, out_uq_slope_t,
    normed_t, kv, kv_t, kv_slope, uq_t, uq_slope_t, w_uq, w_kv, sems,
):
    fetches = [
        pltpu.make_async_copy(w_in.at[:, pl.ds(part * 2 * WIDTH, 2 * WIDTH)], target, sems.at[part])
        for part, target in enumerate((w_uq, w_kv))
    ]
    fetches[1].start()
    fetches[0].start()
    fetches[1].wait()
    for tile in range(TILES):
        rows = pl.ds(tile * TILE, TILE)
        normed, _ = layer_norm_rows(tokens[rows, :].astype(f32))
        normed = (normed * in_gain[...]).astype(bf16)
        project_kv(normed, w_kv, rows, normed_t, kv, kv_t, kv_slope)
    results = [
        pltpu.make_async_copy(source, target, sems.at[2 + at])
        for at, (source, target) in enumerate(
            ((kv, out_kv), (kv_t, out_kv_t), (kv_slope, out_kv_slope), (normed_t, out_normed_t))
        )
    ]
    for copy in results:
        copy.start()
    fetches[0].wait()
    for pair in range(HEADS):
        w_t = w_uq[:, pl.ds(pair * PAIR, PAIR)].T
        both = pl.ds(2 * pair, 2)
        for tile in range(TILES):
            rows = pl.ds(tile * TILE, TILE)
            silu, slope = silu_and_slope(dot(w_t, normed_t[:, rows]))
            uq_t[both, :, rows] = silu.reshape(2, HEAD_DIM, TILE)
            uq_slope_t[both, :, rows] = slope.reshape(2, HEAD_DIM, TILE)
        for source, target in ((uq_t, out_uq_t), (uq_slope_t, out_uq_slope_t)):
            results.append(pltpu.make_async_copy(source.at[both], target.at[both], sems.at[2 + len(results)]))
            results[-1].start()
    for copy in results:
        copy.wait()


VMEM = pl.BlockSpec(memory_space=pltpu.VMEM)
SMEM = pl.BlockSpec(memory_space=pltpu.SMEM)
ANY = pl.BlockSpec(memory_space=pl.ANY)
HBM = pl.BlockSpec(memory_space=pltpu.HBM)


def window_shapes(rows):
    return (
        (WIDTH, rows),
        (2 * HEADS, rows, HEAD_DIM),
        (2 * HEADS, HEAD_DIM, rows),
        (2, rows, WIDTH),
    )


def own_call(*operands):
    along = (2 * HEADS, HEAD_DIM, ROWS)
    shapes = window_shapes(ROWS) + (along, along)
    return pl.pallas_call(
        own_kernel,
        in_specs=[VMEM, VMEM, ANY],
        out_specs=[ANY] * 6,
        out_shape=[jax.ShapeDtypeStruct(shape, bf16) for shape in shapes],
        scratch_shapes=[pltpu.VMEM(shape, bf16) for shape in shapes + ((WIDTH, 2 * WIDTH),) * 2]
        + [pltpu.SemaphoreType.DMA((14,))],
        compiler_params=pltpu.CompilerParams(vmem_limit_bytes=62 * MIB),
        cost_estimate=pl.CostEstimate(
            flops=2 * ROWS * WIDTH * 4 * WIDTH, bytes_accessed=12 * MIB, transcendentals=ROWS * 4 * WIDTH
        ),
        name="own_projection",
    )(*operands)


def relay_kernel(*refs):
    del refs


def slow_relay_call(far, *after):
    return pl.pallas_call(
        relay_kernel,
        in_specs=[ANY] * (1 + len(after)),
        out_specs=ANY,
        out_shape=jax.ShapeDtypeStruct(far.shape, far.dtype),
        input_output_aliases={0: 0},
        cost_estimate=pl.CostEstimate(flops=10*10**9, bytes_accessed=0, transcendentals=0),
        name='relay_home',
    )(far, *after)


def relay_call(far, *after):
    return pl.pallas_call(
        relay_kernel,
        in_specs=[ANY] * (1 + len(after)),
        out_specs=ANY,
        out_shape=jax.ShapeDtypeStruct(far.shape, far.dtype),
        input_output_aliases={0: 0},
        name="relay",
    )(far, *after)


def main_kernel(
    core, in_gain, out_gain, far_ids, near_ids, own_ids,
    far, near_a, near_b, w_in, own_kv, own_uq_t, own_kv_t, own_uq_slope_t, own_w_out, own_cotangent, own_tokens,
    own_normed_t, own_kv_slope,
    out_rows, grad_kv_pre, grad_uq_pre, far_grad, near_grad, mine, theirs,
    normed_t, kv, kv_t, kv_slope, uq_t, uq_slope_t, mask, weights, slopes, mixed_t, grad_attn_t, gated_t, both,
    w_kv, w_out, cotangent, tokens, layer_out, sems,
):
    own = pl.ds(HALO, ROWS)

    def staged(slot, tile):
        return weights.at[slot, :, pl.ds(tile * WIDTH, WIDTH)]

    def starter(source, target):
        copy = pltpu.make_async_copy(source, target, sems.at[len(copies)])
        copies.append(copy)
        copy.start()
        return copy

    copies = []
    starter(w_in.at[:, pl.ds(2 * WIDTH, 2 * WIDTH)], w_kv)
    for slot, source in enumerate((far, near_a, near_b)):
        for tile in range(TILES):
            starter(source.at[pl.ds(tile * TILE, TILE)], staged(slot, tile))
    arrivals = list(copies)
    starter(own_kv, kv.at[:, own, :])
    starter(own_uq_t, uq_t)
    starter(own_kv_t, kv_t.at[:, :, own])
    for_forward = copies[len(arrivals) :]
    starter(own_uq_slope_t, uq_slope_t)
    starter(own_w_out, w_out)
    starter(own_cotangent, cotangent)
    starter(own_tokens, tokens)
    starter(own_normed_t, normed_t.at[:, own])
    starter(own_kv_slope, kv_slope.at[:, own, :])
    for_backward = copies[len(arrivals) + len(for_forward) :]

    key_at = lax.broadcasted_iota(jnp.int32, (TILE, TILE), 0)
    query_at = lax.broadcasted_iota(jnp.int32, (TILE, TILE), 1)
    for key_tile in range(KEY_TILES):
        source = (far_ids, near_ids, own_ids)[key_tile // TILES]
        key_ids = source[:, pl.ds(key_tile % TILES * TILE, TILE)].astype(f32)
        key_ids = jnp.broadcast_to(key_ids, (TILE, TILE)).T
        for tile in query_tiles(key_tile):
            allowed = key_ids == own_ids[:, pl.ds(tile * TILE, TILE)].astype(f32)
            if key_tile == tile:
                allowed = allowed & (key_at > query_at)
            if key_tile == tile + SPREAD - 1:
                allowed = allowed & (key_at <= query_at)
            mask[:, pl.ds(PLACE[key_tile, tile], TILE)] = jnp.where(allowed, 1.0, 0.0).astype(bf16)

    for copy in arrivals:
        copy.wait()
    for tile in range(2 * TILES):
        at = tile % TILES
        if tile < TILES:
            halo = staged(0, at)[...].astype(f32)
        else:
            halo = staged(1, at)[...].astype(f32) + staged(2, at)[...].astype(f32)
        normed, _ = layer_norm_rows(halo)
        normed = (normed * in_gain[...]).astype(bf16)
        project_kv(normed, w_kv, pl.ds(tile * TILE, TILE), normed_t, kv, kv_t, kv_slope)
    for copy in for_forward:
        copy.wait()

    def forward(head, carry):
        for (key_tile, tile), place in PLACE.items():
            band = pl.ds(place, TILE)
            scores = dot(
                kv[head, pl.ds(key_tile * TILE, TILE), :], uq_t[HEADS + head, :, pl.ds(tile * TILE, TILE)]
            )
            half = (scores * HALF_SCALE).astype(bf16)
            tanh = jnp.tanh(half)
            silu = half + half * tanh
            slope = (1.0 + tanh) + silu * (1.0 - tanh)
            keep = mask[:, band]
            weights[head, :, band] = silu * keep
            slopes[head, :, band] = slope * keep
        for tile in range(TILES):
            total = None
            for key_tile in range(tile, tile + SPREAD):
                term = dot(
                    kv_t[HEADS + head, :, pl.ds(key_tile * TILE, TILE)],
                    weights[head, :, pl.ds(PLACE[key_tile, tile], TILE)],
                )
                total = term if total is None else total + term
            mixed_t[head, :, pl.ds(tile * TILE, TILE)] = total
        return carry

    lax.fori_loop(0, HEADS, forward, 0, unroll=True)

    def put(block, value):
        value = value.astype(bf16)
        for part in range(2):
            at = block[part]
            high = jnp.where(at >= HALF_BLOCKS, 1, 0)
            slot = jnp.where(high == core[0], 0, 1)
            both[slot, at - high * HALF_BLOCKS] = value[:, part * HEAD_DIM : (part + 1) * HEAD_DIM]

    for copy in for_backward:
        copy.wait()
    gain = jnp.broadcast_to(out_gain[...], (HEAD_DIM, WIDTH)).T
    gain = jnp.concatenate([gain] * (TILE // HEAD_DIM), axis=1)
    for tile in range(TILES):
        rows = pl.ds(tile * TILE, TILE)
        mixed = mixed_t[:, :, rows].reshape(WIDTH, TILE)
        center = mixed - jnp.mean(mixed, axis=0, keepdims=True)
        inverse = lax.rsqrt(jnp.mean(center * center, axis=0, keepdims=True) + EPSILON)
        normed_out = center * inverse
        scaled_out = normed_out * gain
        u_part = uq_t[pl.ds(0, HEADS), :, rows].reshape(WIDTH, TILE).astype(f32)
        gated = (scaled_out * u_part).astype(bf16)
        gated_t[:, rows] = gated
        upstream = dot_nt(w_out[...], cotangent[rows, :])
        u_slope = uq_slope_t[pl.ds(0, HEADS), :, rows].reshape(WIDTH, TILE).astype(f32)
        grad_u = (upstream * scaled_out * u_slope).astype(bf16)
        uq_slope_t[pl.ds(0, HEADS), :, rows] = grad_u.reshape(HEADS, HEAD_DIM, TILE)
        scaled_grad = upstream * u_part * gain
        first = jnp.mean(scaled_grad, axis=0, keepdims=True)
        second = jnp.mean(scaled_grad * normed_out, axis=0, keepdims=True)
        grad_attn = ((scaled_grad - first - normed_out * second) * inverse).astype(bf16)
        grad_attn_t[:, :, rows] = grad_attn.reshape(HEADS, HEAD_DIM, TILE)
        layer_out[rows, :] = (tokens[rows, :].astype(f32) + dot(gated.T, w_out[...])).astype(bf16)
    for pair in range(HEADS // 2):
        blocks = (2 * pair, 2 * pair + 1)
        columns = pl.ds(pair * PAIR, PAIR)
        put([4 * HEADS + block for block in blocks], dot(gated_t[...], cotangent[:, columns]))
        put(blocks, dot_nt(normed_t[:, own], uq_slope_t[pl.ds(2 * pair, 2)].reshape(PAIR, ROWS)))

    departures = [pltpu.make_async_copy(layer_out, out_rows, sems.at[0])]
    departures[0].start()

    def backward(head, carry):
        columns = pl.ds(pl.multiple_of(head * HEAD_DIM, HEAD_DIM), HEAD_DIM)
        for (key_tile, tile), place in PLACE.items():
            band = pl.ds(place, TILE)
            grad_weights = dot(
                kv[HEADS + head, pl.ds(key_tile * TILE, TILE), :], grad_attn_t[head, :, pl.ds(tile * TILE, TILE)]
            )
            slopes[head, :, band] = grad_weights.astype(bf16) * slopes[head, :, band]
        for key_tile in range(KEY_TILES):
            rows = pl.ds(key_tile * TILE, TILE)
            span = query_tiles(key_tile)
            band = pl.ds(PLACE[key_tile, span[0]], len(span) * TILE)
            queries = pl.ds(span[0] * TILE, len(span) * TILE)
            grad_keys = dot_nt(slopes[head, :, band], uq_t[HEADS + head, :, queries])
            grad_values = dot_nt(weights[head, :, band], grad_attn_t[head, :, queries])
            slope = kv_slope[0, rows, columns].astype(f32)
            kv_slope[0, rows, columns] = (grad_keys * slope * HALF_SCALE).astype(bf16)
            slope = kv_slope[1, rows, columns].astype(f32)
            kv_slope[1, rows, columns] = (grad_values * slope).astype(bf16)
        for tile in range(TILES):
            total = None
            for key_tile in range(tile, tile + SPREAD):
                term = dot(
                    kv_t[head, :, pl.ds(key_tile * TILE, TILE)],
                    slopes[head, :, pl.ds(PLACE[key_tile, tile], TILE)],
                )
                total = term if total is None else total + term
            queries = pl.ds(tile * TILE, TILE)
            slope = uq_slope_t[HEADS + head, :, queries].astype(f32)
            uq_slope_t[HEADS + head, :, queries] = (total * slope * HALF_SCALE).astype(bf16)
        return carry

    lax.fori_loop(0, HEADS, backward, 0, unroll=True)

    def depart(source, target):
        departures.append(pltpu.make_async_copy(source, target, sems.at[len(departures)]))
        departures[-1].start()

    def half_done(half):
        at = len(departures)
        departures.append(pltpu.make_async_copy(both.at[0], mine, sems.at[at]))

        @pl.when(core[0] == half)
        def _():
            pltpu.make_async_copy(both.at[0], mine, sems.at[at]).start()

        @pl.when(core[0] != half)
        def _():
            pltpu.make_async_copy(both.at[1], theirs, sems.at[at]).start()

    def put_pair(part, pair):
        blocks = [part * HEADS + 2 * pair + which for which in range(2)]
        columns = pl.ds(pair * PAIR, PAIR)
        if part == 1:
            queries = uq_slope_t[pl.ds(HEADS + 2 * pair, 2)].reshape(PAIR, ROWS)
            put(blocks, dot_nt(normed_t[:, own], queries))
        else:
            put(blocks, dot(normed_t[...], kv_slope[part - 2, :, columns]))

    for tile in range(2 * TILES):
        rows = pl.ds(tile * TILE, TILE)
        total = sum(dot_nt(kv_slope[part, rows, :], w_kv[:, pl.ds(part * WIDTH, WIDTH)]) for part in range(2))
        slot, at = divmod(tile, TILES)
        staged(slot, at)[...] = total.astype(bf16)
        depart(staged(slot, at), (far_grad, near_grad)[slot].at[pl.ds(at * TILE, TILE)])
    depart(kv_slope.at[:, own, :], grad_kv_pre)
    depart(uq_slope_t, grad_uq_pre)
    for part, pair in ((1, 0), (1, 1), (2, 0)):
        put_pair(part, pair)
    half_done(0)
    for part, pair in ((2, 1), (3, 0), (3, 1)):
        put_pair(part, pair)
    half_done(1)
    for copy in departures:
        copy.wait()


def main_call(*operands):
    along = (2 * HEADS, HEAD_DIM, ROWS)
    half = (HALF_BLOCKS, WIDTH, HEAD_DIM)
    scratch = [pltpu.VMEM(shape, bf16) for shape in window_shapes(WINDOW_ROWS)] + [
        pltpu.VMEM(along, bf16),
        pltpu.VMEM(along, bf16),
        pltpu.VMEM((TILE, BAND), bf16),
        pltpu.VMEM((HEADS, TILE, BAND), bf16),
        pltpu.VMEM((HEADS, TILE, BAND), bf16),
        pltpu.VMEM((HEADS, HEAD_DIM, ROWS), f32),
        pltpu.VMEM((HEADS, HEAD_DIM, ROWS), bf16),
        pltpu.VMEM((WIDTH, ROWS), bf16),
        pltpu.VMEM((2,) + half, bf16),
        pltpu.VMEM((WIDTH, 2 * WIDTH), bf16),
        pltpu.VMEM((WIDTH, WIDTH), bf16),
        pltpu.VMEM((ROWS, WIDTH), bf16),
        pltpu.VMEM((ROWS, WIDTH), bf16),
        pltpu.VMEM((ROWS, WIDTH), bf16),
        pltpu.SemaphoreType.DMA((20,)),
    ]
    return pl.pallas_call(
        main_kernel,
        in_specs=[SMEM] + [VMEM] * 5 + [ANY] * (len(operands) - 6),
        out_specs=[ANY] * 7,
        out_shape=[
            jax.ShapeDtypeStruct(shape, bf16)
            for shape in ((ROWS, WIDTH), (2, ROWS, WIDTH), along, (ROWS, WIDTH), (ROWS, WIDTH), half, half)
        ],
        scratch_shapes=scratch,
        compiler_params=pltpu.CompilerParams(vmem_limit_bytes=62 * MIB),
        cost_estimate=pl.CostEstimate(flops=20 * 10**9, bytes_accessed=24 * MIB, transcendentals=6 * 10**6),
        name="attention",
    )(*operands)


def back_kernel(grad_kv_pre, grad_uq_pre, w_in, after, grad_normed):
    del after
    across = dot(w_in[:, pl.ds(0, 2 * WIDTH)], grad_uq_pre[...].reshape(2 * WIDTH, ROWS))
    along = sum(dot_nt(grad_kv_pre[part], w_in[:, pl.ds((2 + part) * WIDTH, WIDTH)]) for part in range(2))
    grad_normed[...] = across.T + along


def back_call(*operands):
    return pl.pallas_call(
        back_kernel,
        in_specs=[VMEM] * 3 + [ANY],
        out_specs=VMEM,
        out_shape=jax.ShapeDtypeStruct((ROWS, WIDTH), f32),
        compiler_params=pltpu.CompilerParams(vmem_limit_bytes=24 * MIB),
        cost_estimate=pl.CostEstimate(flops=16 * 10**8, bytes_accessed=8 * MIB, transcendentals=0),
        name="projection_gradient",
    )(*operands)


PIECES = 4


def pair_kernel(core, mine, arrived, far_grad, swapped, total, out_a, out_b, held, others, homes, nears, sems, out_sems):
    rows = HALF_BLOCKS * WIDTH // PIECES
    home_rows = ROWS // 2
    copies = []

    def start(source, target):
        copies.append(pltpu.make_async_copy(source, target, sems.at[len(copies)]))
        copies[-1].start()

    for half in range(2):
        at = pl.ds(half * home_rows, home_rows)
        start(far_grad.at[at], homes.at[at])
        start(swapped.at[at], nears.at[at])
    for piece in range(PIECES):
        at = pl.ds(piece * rows, rows)
        start(mine.at[at], held.at[at])
        start(arrived.at[at], others.at[at])
    results = []

    def finish(source, target):
        results.append(pltpu.make_async_copy(source, target, out_sems.at[len(results)]))
        results[-1].start()

    for half, target in enumerate((out_a, out_b)):
        at = pl.ds(half * home_rows, home_rows)
        copies[2 * half].wait()
        copies[2 * half + 1].wait()
        near = jnp.where(core[0] == 1, nears[at, :].astype(f32), 0.0)
        homes[at, :] = (homes[at, :].astype(f32) + near).astype(bf16)
        finish(homes.at[at], target)
    for piece in range(PIECES):
        at = pl.ds(piece * rows, rows)
        copies[4 + 2 * piece].wait()
        copies[5 + 2 * piece].wait()
        held[at, :] = (held[at, :].astype(f32) + others[at, :].astype(f32)).astype(bf16)
        finish(held.at[at], total.at[at])
    for copy in results:
        copy.wait()


def pair_call(core, *operands):
    half = (HALF_BLOCKS * WIDTH, HEAD_DIM)
    home = (ROWS, WIDTH)
    return pl.pallas_call(
        pair_kernel,
        in_specs=[SMEM] + [ANY] * 4,
        out_specs=[ANY] * 3,
        out_shape=[jax.ShapeDtypeStruct(shape, bf16) for shape in (half, (ROWS // 2, WIDTH), (ROWS // 2, WIDTH))],
        scratch_shapes=[pltpu.VMEM(shape, bf16) for shape in (half, half, home, home)]
        + [pltpu.SemaphoreType.DMA((4 + 2 * PIECES,)), pltpu.SemaphoreType.DMA((2 + PIECES,))],
        compiler_params=pltpu.CompilerParams(vmem_limit_bytes=62 * MIB),
        name="pair_sum",
    )(core, *operands)


def chips_kernel(parts, *refs):
    totals = refs[-1]
    total = jnp.sum(parts[...].astype(f32), axis=0, keepdims=True).astype(bf16)
    totals[...] = jnp.broadcast_to(total, totals.shape)


def chips_call(parts, *after):
    return pl.pallas_call(
        chips_kernel,
        in_specs=[VMEM] + [ANY] * len(after),
        out_specs=VMEM,
        out_shape=jax.ShapeDtypeStruct(parts.shape, bf16),
        compiler_params=pltpu.CompilerParams(vmem_limit_bytes=24 * MIB),
        name="chip_sum",
    )(parts, *after)


def unpack_kernel(flip, core, blocks, *refs):
    grad_w_in, grad_w_out, staging, sems = refs[-4:]
    for half in range(2):

        @pl.when(core[0] == half ^ flip)
        def _(half=half):
            copies = []
            for at in range(HALF_BLOCKS):
                staging[at] = blocks[at].astype(f32)
                block = half * HALF_BLOCKS + at
                if block < 4 * HEADS:
                    target = grad_w_in.at[:, pl.ds(block * HEAD_DIM, HEAD_DIM)]
                else:
                    target = grad_w_out.at[:, pl.ds((block - 4 * HEADS) * HEAD_DIM, HEAD_DIM)]
                copies.append(pltpu.make_async_copy(staging.at[at], target, sems.at[at]))
                copies[-1].start()
            for copy in copies:
                copy.wait()


def unpack_call(core, blocks, flip, into=()):
    return pl.pallas_call(
        functools.partial(unpack_kernel, flip),
        in_specs=[SMEM, VMEM] + [ANY] * len(into),
        out_specs=[ANY] * 2,
        out_shape=(
            jax.ShapeDtypeStruct((WIDTH, 4 * WIDTH), f32),
            jax.ShapeDtypeStruct((WIDTH, WIDTH), f32),
        ),
        scratch_shapes=[
            pltpu.VMEM((HALF_BLOCKS, WIDTH, HEAD_DIM), f32),
            pltpu.SemaphoreType.DMA((HALF_BLOCKS,)),
        ],
        input_output_aliases={2: 0, 3: 1} if into else {},
        compiler_params=pltpu.CompilerParams(vmem_limit_bytes=24 * MIB),
        cost_estimate=pl.CostEstimate(flops=4 * 10**9, bytes_accessed=4 * MIB, transcendentals=0),
        name="unpack",
    )(core, blocks, *into)


def step_kernel(
    core, in_gain, tokens, cotangent, grad_normed, sent_a, sent_b, swapped, after, grad_tokens,
    rows_in, cot, grad, sent, near, result, sems, out_sems,
):
    del after
    half = ROWS // 2
    copies = []
    for part, sent_half in enumerate((sent_a, sent_b)):
        at = pl.ds(part * half, half)
        for source, target in (
            (tokens.at[at], rows_in.at[at]),
            (grad_normed.at[at], grad.at[at]),
            (swapped.at[at], near.at[at]),
            (sent_half, sent.at[at]),
            (cotangent.at[at], cot.at[at]),
        ):
            copies.append(pltpu.make_async_copy(source, target, sems.at[len(copies)]))
            copies[-1].start()
    results = []
    for part in range(2):
        at = pl.ds(part * half, half)
        copies[5 * part].wait()
        normed, inverse = layer_norm_rows(rows_in[at, :].astype(f32))
        for copy in copies[5 * part + 1 : 5 * part + 5]:
            copy.wait()
        home = jnp.where(core[0] == 0, near[at, :].astype(f32), 0.0)
        scaled_grad = (grad[at, :] + sent[at, :].astype(f32) + home) * in_gain[...]
        first = jnp.mean(scaled_grad, axis=1, keepdims=True)
        second = jnp.mean(scaled_grad * normed, axis=1, keepdims=True)
        result[at, :] = (
            cot[at, :].astype(f32) + (scaled_grad - first - normed * second) * inverse
        ).astype(bf16)
        results.append(pltpu.make_async_copy(result.at[at], grad_tokens.at[at], out_sems.at[part]))
        results[-1].start()
    for copy in results:
        copy.wait()


def step_call(*operands):
    shape = (ROWS, WIDTH)
    return pl.pallas_call(
        step_kernel,
        in_specs=[SMEM, VMEM] + [ANY] * 7,
        out_specs=ANY,
        out_shape=jax.ShapeDtypeStruct(shape, bf16),
        scratch_shapes=[pltpu.VMEM(shape, kind) for kind in (bf16, bf16, f32, bf16, bf16, bf16)]
        + [pltpu.SemaphoreType.DMA((10,)), pltpu.SemaphoreType.DMA((2,))],
        compiler_params=pltpu.CompilerParams(vmem_limit_bytes=62 * MIB),
        name="input_norm_gradient",
    )(*operands)


def shifted(value, steps):
    count = 128
    first, last = (max(0, -steps), min(count, count - steps))
    return lax.ppermute(value, ALL, [(source, source + steps) for source in range(first, last)])


SWAP = [(0, 1), (1, 0)]


def on_device(tokens, user_ids, in_gain, out_gain, w_in, w_out, cotangent):
    core = lax.axis_index("core").astype(jnp.int32).reshape(1)
    in_gain_row = in_gain.reshape(1, WIDTH)
    own_ids = user_ids.reshape(1, ROWS)

    far = shifted(tokens, 2)
    near_a = lax.ppermute(tokens, "core", [(0, 1)])
    far_ids = shifted(own_ids, 2)
    near_ids = shifted(own_ids, 1)
    *window, uq_t, uq_slope_t = own_call(tokens, in_gain_row, w_in)
    far = relay_call(far, uq_t, far_ids, near_ids)
    near_b = lax.ppermute(far, "core", [(1, 0)])
    normed_t, kv, kv_t, kv_slope = window
    layer_out, grad_kv_pre, grad_uq_pre, far_grad, near_grad, mine, theirs = main_call(
        core, in_gain_row, out_gain.reshape(1, WIDTH), far_ids, near_ids, own_ids,
        far, near_a, near_b, w_in, kv, uq_t, kv_t, uq_slope_t, w_out, cotangent, tokens, normed_t, kv_slope,
    )

    arrived = lax.ppermute(theirs, "core", SWAP)
    swapped = lax.ppermute(near_grad, "core", SWAP)
    flat = (HALF_BLOCKS * WIDTH, HEAD_DIM)
    partial, out_a, out_b = pair_call(core, mine.reshape(flat), arrived.reshape(flat), far_grad, swapped)
    sent_a = slow_relay_call(shifted(out_a, -2))
    grad_normed = back_call(grad_kv_pre, grad_uq_pre, w_in, out_b)
    parts = lax.all_to_all(partial.reshape(64, 80, HEAD_DIM), CHIPS, 0, 0, tiled=True)
    totals = lax.all_to_all(chips_call(parts, grad_normed, sent_a), CHIPS, 0, 0, tiled=True)
    totals = totals.reshape(HALF_BLOCKS, WIDTH, HEAD_DIM)
    other = lax.ppermute(totals, "core", SWAP)
    halves = unpack_call(core, totals, 0)
    sent_b = slow_relay_call(shifted(out_b, -2), halves[1])
    grad_w_in, grad_w_out = unpack_call(core, other, 1, halves)
    grad_tokens = step_call(
        core, in_gain_row, tokens, cotangent, grad_normed, sent_a, sent_b, swapped, grad_w_out,
    )
    return (layer_out, grad_tokens, grad_w_in, grad_w_out)


def solution(mesh):
    fine = Mesh(mesh.devices.reshape(2, 4, 2, 4, 2), ALL)
    placed = (P(ALL, None), P(ALL), P(), P(), P(), P(), P(ALL, None))
    return jax.shard_map(
        on_device,
        mesh=fine,
        in_specs=placed,
        out_specs=(P(ALL, None), P(ALL, None), P(), P()),
        check_vma=False,
    )
```

```python
import functools

import jax
import jax.numpy as jnp
from jax import lax
from jax.experimental import pallas as pl
from jax.experimental.pallas import tpu as pltpu
from jax.sharding import Mesh
from jax.sharding import PartitionSpec as P

HEADS = 4
HEAD_DIM = 128
ROWS = 768
WIDTH = 512
WINDOW_ROWS = 3 * ROWS
HALO = 2 * ROWS
TILE = 256
TILES = ROWS // TILE
SPREAD = 7
PAIR = 2 * HEAD_DIM
KEY_TILES = WINDOW_ROWS // TILE
HALF_SCALE = 0.5 * HEAD_DIM ** (-0.5)
EPSILON = 1e-05
BLOCKS = 5 * HEADS
HALF_BLOCKS = BLOCKS // 2

ALL = ("z_hi", "y", "z_lo", "x", "core")
CHIPS = ("z_hi", "y", "z_lo", "x")
MIB = 1024 * 1024

f32 = jnp.float32
bf16 = jnp.bfloat16


def dot(left, right):
    return lax.dot_general(left, right, (((1,), (0,)), ((), ())), preferred_element_type=f32)


def dot_nt(left, right):
    return lax.dot_general(left, right, (((1,), (1,)), ((), ())), preferred_element_type=f32)


def layer_norm_rows(values):
    center = values - jnp.mean(values, axis=1, keepdims=True)
    inverse = lax.rsqrt(jnp.mean(center * center, axis=1, keepdims=True) + EPSILON)
    return center * inverse, inverse


def silu_and_slope(value):
    half = 0.5 * value
    tanh = jnp.tanh(half)
    silu = (half + half * tanh).astype(bf16)
    tanh = tanh.astype(bf16)
    slope = 0.5 * ((1.0 + tanh) + silu * (1.0 - tanh))
    return silu, slope


def first_query_tile(key_tile):
    return max(0, key_tile - SPREAD + 1)


def query_tiles(key_tile):
    return range(first_query_tile(key_tile), min(TILES, key_tile + 1))


PLACE = {}
for _key_tile in range(KEY_TILES):
    for _tile in query_tiles(_key_tile):
        PLACE[_key_tile, _tile] = len(PLACE) * TILE
BAND = len(PLACE) * TILE


def project_kv(normed, w_kv, rows, normed_t, kv, kv_t, kv_slope):
    normed_t[:, rows] = normed.T
    for part in range(2):
        for pair in range(HEADS // 2):
            columns = pl.ds(part * WIDTH + pair * PAIR, PAIR)
            silu, slope = silu_and_slope(dot(normed, w_kv[:, columns]))
            kv_slope[part, rows, pl.ds(pair * PAIR, PAIR)] = slope
            for which in range(2):
                head = 2 * pair + which
                lanes = slice(which * HEAD_DIM, (which + 1) * HEAD_DIM)
                kv[part * HEADS + head, rows, :] = silu[:, lanes]
                kv_t[part * HEADS + head, :, rows] = silu[:, lanes].T


def own_kernel(
    tokens, in_gain, w_in, out_normed_t, out_kv, out_kv_t, out_kv_slope, out_uq_t, out_uq_slope_t,
    normed_t, kv, kv_t, kv_slope, uq_t, uq_slope_t, w_uq, w_kv, sems,
):
    fetches = [
        pltpu.make_async_copy(w_in.at[:, pl.ds(part * 2 * WIDTH, 2 * WIDTH)], target, sems.at[part])
        for part, target in enumerate((w_uq, w_kv))
    ]
    fetches[1].start()
    fetches[0].start()
    fetches[1].wait()
    for tile in range(TILES):
        rows = pl.ds(tile * TILE, TILE)
        normed, _ = layer_norm_rows(tokens[rows, :].astype(f32))
        normed = (normed * in_gain[...]).astype(bf16)
        project_kv(normed, w_kv, rows, normed_t, kv, kv_t, kv_slope)
    results = [
        pltpu.make_async_copy(source, target, sems.at[2 + at])
        for at, (source, target) in enumerate(
            ((kv, out_kv), (kv_t, out_kv_t), (kv_slope, out_kv_slope), (normed_t, out_normed_t))
        )
    ]
    for copy in results:
        copy.start()
    fetches[0].wait()
    for pair in range(HEADS):
        w_t = w_uq[:, pl.ds(pair * PAIR, PAIR)].T
        both = pl.ds(2 * pair, 2)
        for tile in range(TILES):
            rows = pl.ds(tile * TILE, TILE)
            silu, slope = silu_and_slope(dot(w_t, normed_t[:, rows]))
            uq_t[both, :, rows] = silu.reshape(2, HEAD_DIM, TILE)
            uq_slope_t[both, :, rows] = slope.reshape(2, HEAD_DIM, TILE)
        for source, target in ((uq_t, out_uq_t), (uq_slope_t, out_uq_slope_t)):
            results.append(pltpu.make_async_copy(source.at[both], target.at[both], sems.at[2 + len(results)]))
            results[-1].start()
    for copy in results:
        copy.wait()


VMEM = pl.BlockSpec(memory_space=pltpu.VMEM)
SMEM = pl.BlockSpec(memory_space=pltpu.SMEM)
ANY = pl.BlockSpec(memory_space=pl.ANY)
HBM = pl.BlockSpec(memory_space=pltpu.HBM)


def window_shapes(rows):
    return (
        (WIDTH, rows),
        (2 * HEADS, rows, HEAD_DIM),
        (2 * HEADS, HEAD_DIM, rows),
        (2, rows, WIDTH),
    )


def own_call(*operands):
    along = (2 * HEADS, HEAD_DIM, ROWS)
    shapes = window_shapes(ROWS) + (along, along)
    return pl.pallas_call(
        own_kernel,
        in_specs=[VMEM, VMEM, ANY],
        out_specs=[ANY] * 6,
        out_shape=[jax.ShapeDtypeStruct(shape, bf16) for shape in shapes],
        scratch_shapes=[pltpu.VMEM(shape, bf16) for shape in shapes + ((WIDTH, 2 * WIDTH),) * 2]
        + [pltpu.SemaphoreType.DMA((14,))],
        compiler_params=pltpu.CompilerParams(vmem_limit_bytes=62 * MIB),
        cost_estimate=pl.CostEstimate(
            flops=2 * ROWS * WIDTH * 4 * WIDTH, bytes_accessed=12 * MIB, transcendentals=ROWS * 4 * WIDTH
        ),
        name="own_projection",
    )(*operands)


def relay_kernel(*refs):
    del refs


def slow_relay_call(far, *after):
    return pl.pallas_call(
        relay_kernel,
        in_specs=[ANY] * (1 + len(after)),
        out_specs=ANY,
        out_shape=jax.ShapeDtypeStruct(far.shape, far.dtype),
        input_output_aliases={0: 0},
        cost_estimate=pl.CostEstimate(flops=10*10**9, bytes_accessed=0, transcendentals=0),
        name='relay_home',
    )(far, *after)


def relay_call(far, *after):
    return pl.pallas_call(
        relay_kernel,
        in_specs=[ANY] * (1 + len(after)),
        out_specs=ANY,
        out_shape=jax.ShapeDtypeStruct(far.shape, far.dtype),
        input_output_aliases={0: 0},
        name="relay",
    )(far, *after)


def main_kernel(
    core, in_gain, out_gain, far_ids, near_ids, own_ids,
    far, near_a, near_b, w_in, own_kv, own_uq_t, own_kv_t, own_uq_slope_t, own_w_out, own_cotangent, own_tokens,
    own_normed_t, own_kv_slope,
    out_rows, grad_kv_pre, grad_uq_pre, far_grad, near_grad, mine, theirs,
    normed_t, kv, kv_t, kv_slope, uq_t, uq_slope_t, mask, weights, slopes, mixed_t, grad_attn_t, gated_t, both,
    w_kv, w_out, cotangent, tokens, layer_out, sems,
):
    own = pl.ds(HALO, ROWS)

    def staged(slot, tile):
        return weights.at[slot, :, pl.ds(tile * WIDTH, WIDTH)]

    def starter(source, target):
        copy = pltpu.make_async_copy(source, target, sems.at[len(copies)])
        copies.append(copy)
        copy.start()
        return copy

    copies = []
    starter(w_in.at[:, pl.ds(2 * WIDTH, 2 * WIDTH)], w_kv)
    for slot, source in enumerate((far, near_a, near_b)):
        for tile in range(TILES):
            starter(source.at[pl.ds(tile * TILE, TILE)], staged(slot, tile))
    arrivals = list(copies)
    starter(own_kv, kv.at[:, own, :])
    starter(own_uq_t, uq_t)
    starter(own_kv_t, kv_t.at[:, :, own])
    for_forward = copies[len(arrivals) :]
    starter(own_uq_slope_t, uq_slope_t)
    starter(own_w_out, w_out)
    starter(own_cotangent, cotangent)
    starter(own_tokens, tokens)
    starter(own_normed_t, normed_t.at[:, own])
    starter(own_kv_slope, kv_slope.at[:, own, :])
    for_backward = copies[len(arrivals) + len(for_forward) :]

    key_at = lax.broadcasted_iota(jnp.int32, (TILE, TILE), 0)
    query_at = lax.broadcasted_iota(jnp.int32, (TILE, TILE), 1)
    for key_tile in range(KEY_TILES):
        source = (far_ids, near_ids, own_ids)[key_tile // TILES]
        key_ids = source[:, pl.ds(key_tile % TILES * TILE, TILE)].astype(f32)
        key_ids = jnp.broadcast_to(key_ids, (TILE, TILE)).T
        for tile in query_tiles(key_tile):
            allowed = key_ids == own_ids[:, pl.ds(tile * TILE, TILE)].astype(f32)
            if key_tile == tile:
                allowed = allowed & (key_at > query_at)
            if key_tile == tile + SPREAD - 1:
                allowed = allowed & (key_at <= query_at)
            mask[:, pl.ds(PLACE[key_tile, tile], TILE)] = jnp.where(allowed, 1.0, 0.0).astype(bf16)

    for copy in arrivals:
        copy.wait()
    for tile in range(2 * TILES):
        at = tile % TILES
        if tile < TILES:
            halo = staged(0, at)[...].astype(f32)
        else:
            halo = staged(1, at)[...].astype(f32) + staged(2, at)[...].astype(f32)
        normed, _ = layer_norm_rows(halo)
        normed = (normed * in_gain[...]).astype(bf16)
        project_kv(normed, w_kv, pl.ds(tile * TILE, TILE), normed_t, kv, kv_t, kv_slope)
    for copy in for_forward:
        copy.wait()

    def forward(head, carry):
        for (key_tile, tile), place in PLACE.items():
            band = pl.ds(place, TILE)
            scores = dot(
                kv[head, pl.ds(key_tile * TILE, TILE), :], uq_t[HEADS + head, :, pl.ds(tile * TILE, TILE)]
            )
            half = (scores * HALF_SCALE).astype(bf16)
            tanh = jnp.tanh(half)
            silu = half + half * tanh
            slope = (1.0 + tanh) + silu * (1.0 - tanh)
            keep = mask[:, band]
            weights[head, :, band] = silu * keep
            slopes[head, :, band] = slope * keep
        for tile in range(TILES):
            total = None
            for key_tile in range(tile, tile + SPREAD):
                term = dot(
                    kv_t[HEADS + head, :, pl.ds(key_tile * TILE, TILE)],
                    weights[head, :, pl.ds(PLACE[key_tile, tile], TILE)],
                )
                total = term if total is None else total + term
            mixed_t[head, :, pl.ds(tile * TILE, TILE)] = total
        return carry

    lax.fori_loop(0, HEADS, forward, 0, unroll=2)

    def put(block, value):
        value = value.astype(bf16)
        for part in range(2):
            at = block[part]
            high = jnp.where(at >= HALF_BLOCKS, 1, 0)
            slot = jnp.where(high == core[0], 0, 1)
            both[slot, at - high * HALF_BLOCKS] = value[:, part * HEAD_DIM : (part + 1) * HEAD_DIM]

    for copy in for_backward:
        copy.wait()
    gain = jnp.broadcast_to(out_gain[...], (HEAD_DIM, WIDTH)).T
    gain = jnp.concatenate([gain] * (TILE // HEAD_DIM), axis=1)
    for tile in range(TILES):
        rows = pl.ds(tile * TILE, TILE)
        mixed = mixed_t[:, :, rows].reshape(WIDTH, TILE)
        center = mixed - jnp.mean(mixed, axis=0, keepdims=True)
        inverse = lax.rsqrt(jnp.mean(center * center, axis=0, keepdims=True) + EPSILON)
        normed_out = center * inverse
        scaled_out = normed_out * gain
        u_part = uq_t[pl.ds(0, HEADS), :, rows].reshape(WIDTH, TILE).astype(f32)
        gated = (scaled_out * u_part).astype(bf16)
        gated_t[:, rows] = gated
        upstream = dot_nt(w_out[...], cotangent[rows, :])
        u_slope = uq_slope_t[pl.ds(0, HEADS), :, rows].reshape(WIDTH, TILE).astype(f32)
        grad_u = (upstream * scaled_out * u_slope).astype(bf16)
        uq_slope_t[pl.ds(0, HEADS), :, rows] = grad_u.reshape(HEADS, HEAD_DIM, TILE)
        scaled_grad = upstream * u_part * gain
        first = jnp.mean(scaled_grad, axis=0, keepdims=True)
        second = jnp.mean(scaled_grad * normed_out, axis=0, keepdims=True)
        grad_attn = ((scaled_grad - first - normed_out * second) * inverse).astype(bf16)
        grad_attn_t[:, :, rows] = grad_attn.reshape(HEADS, HEAD_DIM, TILE)
        layer_out[rows, :] = (tokens[rows, :].astype(f32) + dot(gated.T, w_out[...])).astype(bf16)
    for pair in range(HEADS // 2):
        blocks = (2 * pair, 2 * pair + 1)
        columns = pl.ds(pair * PAIR, PAIR)
        put([4 * HEADS + block for block in blocks], dot(gated_t[...], cotangent[:, columns]))
        put(blocks, dot_nt(normed_t[:, own], uq_slope_t[pl.ds(2 * pair, 2)].reshape(PAIR, ROWS)))

    departures = [pltpu.make_async_copy(layer_out, out_rows, sems.at[0])]
    departures[0].start()

    def backward(head, carry):
        columns = pl.ds(pl.multiple_of(head * HEAD_DIM, HEAD_DIM), HEAD_DIM)
        for (key_tile, tile), place in PLACE.items():
            band = pl.ds(place, TILE)
            grad_weights = dot(
                kv[HEADS + head, pl.ds(key_tile * TILE, TILE), :], grad_attn_t[head, :, pl.ds(tile * TILE, TILE)]
            )
            slopes[head, :, band] = grad_weights.astype(bf16) * slopes[head, :, band]
        for key_tile in range(KEY_TILES):
            rows = pl.ds(key_tile * TILE, TILE)
            span = query_tiles(key_tile)
            band = pl.ds(PLACE[key_tile, span[0]], len(span) * TILE)
            queries = pl.ds(span[0] * TILE, len(span) * TILE)
            grad_keys = dot_nt(slopes[head, :, band], uq_t[HEADS + head, :, queries])
            grad_values = dot_nt(weights[head, :, band], grad_attn_t[head, :, queries])
            slope = kv_slope[0, rows, columns].astype(f32)
            kv_slope[0, rows, columns] = (grad_keys * slope * HALF_SCALE).astype(bf16)
            slope = kv_slope[1, rows, columns].astype(f32)
            kv_slope[1, rows, columns] = (grad_values * slope).astype(bf16)
        for tile in range(TILES):
            total = None
            for key_tile in range(tile, tile + SPREAD):
                term = dot(
                    kv_t[head, :, pl.ds(key_tile * TILE, TILE)],
                    slopes[head, :, pl.ds(PLACE[key_tile, tile], TILE)],
                )
                total = term if total is None else total + term
            queries = pl.ds(tile * TILE, TILE)
            slope = uq_slope_t[HEADS + head, :, queries].astype(f32)
            uq_slope_t[HEADS + head, :, queries] = (total * slope * HALF_SCALE).astype(bf16)
        return carry

    lax.fori_loop(0, HEADS, backward, 0, unroll=2)

    def depart(source, target):
        departures.append(pltpu.make_async_copy(source, target, sems.at[len(departures)]))
        departures[-1].start()

    def half_done(half):
        at = len(departures)
        departures.append(pltpu.make_async_copy(both.at[0], mine, sems.at[at]))

        @pl.when(core[0] == half)
        def _():
            pltpu.make_async_copy(both.at[0], mine, sems.at[at]).start()

        @pl.when(core[0] != half)
        def _():
            pltpu.make_async_copy(both.at[1], theirs, sems.at[at]).start()

    def put_pair(part, pair):
        blocks = [part * HEADS + 2 * pair + which for which in range(2)]
        columns = pl.ds(pair * PAIR, PAIR)
        if part == 1:
            queries = uq_slope_t[pl.ds(HEADS + 2 * pair, 2)].reshape(PAIR, ROWS)
            put(blocks, dot_nt(normed_t[:, own], queries))
        else:
            put(blocks, dot(normed_t[...], kv_slope[part - 2, :, columns]))

    for tile in range(2 * TILES):
        rows = pl.ds(tile * TILE, TILE)
        total = sum(dot_nt(kv_slope[part, rows, :], w_kv[:, pl.ds(part * WIDTH, WIDTH)]) for part in range(2))
        slot, at = divmod(tile, TILES)
        staged(slot, at)[...] = total.astype(bf16)
        depart(staged(slot, at), (far_grad, near_grad)[slot].at[pl.ds(at * TILE, TILE)])
    depart(kv_slope.at[:, own, :], grad_kv_pre)
    depart(uq_slope_t, grad_uq_pre)
    for part, pair in ((1, 0), (1, 1), (2, 0)):
        put_pair(part, pair)
    half_done(0)
    for part, pair in ((2, 1), (3, 0), (3, 1)):
        put_pair(part, pair)
    half_done(1)
    for copy in departures:
        copy.wait()


def main_call(*operands):
    along = (2 * HEADS, HEAD_DIM, ROWS)
    half = (HALF_BLOCKS, WIDTH, HEAD_DIM)
    scratch = [pltpu.VMEM(shape, bf16) for shape in window_shapes(WINDOW_ROWS)] + [
        pltpu.VMEM(along, bf16),
        pltpu.VMEM(along, bf16),
        pltpu.VMEM((TILE, BAND), bf16),
        pltpu.VMEM((HEADS, TILE, BAND), bf16),
        pltpu.VMEM((HEADS, TILE, BAND), bf16),
        pltpu.VMEM((HEADS, HEAD_DIM, ROWS), f32),
        pltpu.VMEM((HEADS, HEAD_DIM, ROWS), bf16),
        pltpu.VMEM((WIDTH, ROWS), bf16),
        pltpu.VMEM((2,) + half, bf16),
        pltpu.VMEM((WIDTH, 2 * WIDTH), bf16),
        pltpu.VMEM((WIDTH, WIDTH), bf16),
        pltpu.VMEM((ROWS, WIDTH), bf16),
        pltpu.VMEM((ROWS, WIDTH), bf16),
        pltpu.VMEM((ROWS, WIDTH), bf16),
        pltpu.SemaphoreType.DMA((20,)),
    ]
    return pl.pallas_call(
        main_kernel,
        in_specs=[SMEM] + [VMEM] * 5 + [ANY] * (len(operands) - 6),
        out_specs=[ANY] * 7,
        out_shape=[
            jax.ShapeDtypeStruct(shape, bf16)
            for shape in ((ROWS, WIDTH), (2, ROWS, WIDTH), along, (ROWS, WIDTH), (ROWS, WIDTH), half, half)
        ],
        scratch_shapes=scratch,
        compiler_params=pltpu.CompilerParams(vmem_limit_bytes=62 * MIB),
        cost_estimate=pl.CostEstimate(flops=20 * 10**9, bytes_accessed=24 * MIB, transcendentals=6 * 10**6),
        name="attention",
    )(*operands)


def back_kernel(grad_kv_pre, grad_uq_pre, w_in, after, grad_normed):
    del after
    across = dot(w_in[:, pl.ds(0, 2 * WIDTH)], grad_uq_pre[...].reshape(2 * WIDTH, ROWS))
    along = sum(dot_nt(grad_kv_pre[part], w_in[:, pl.ds((2 + part) * WIDTH, WIDTH)]) for part in range(2))
    grad_normed[...] = across.T + along


def back_call(*operands):
    return pl.pallas_call(
        back_kernel,
        in_specs=[VMEM] * 3 + [ANY],
        out_specs=VMEM,
        out_shape=jax.ShapeDtypeStruct((ROWS, WIDTH), f32),
        compiler_params=pltpu.CompilerParams(vmem_limit_bytes=24 * MIB),
        cost_estimate=pl.CostEstimate(flops=16 * 10**8, bytes_accessed=8 * MIB, transcendentals=0),
        name="projection_gradient",
    )(*operands)


PIECES = 4


def pair_kernel(core, mine, arrived, far_grad, swapped, total, out_a, out_b, held, others, homes, nears, sems, out_sems):
    rows = HALF_BLOCKS * WIDTH // PIECES
    home_rows = ROWS // 2
    copies = []

    def start(source, target):
        copies.append(pltpu.make_async_copy(source, target, sems.at[len(copies)]))
        copies[-1].start()

    for half in range(2):
        at = pl.ds(half * home_rows, home_rows)
        start(far_grad.at[at], homes.at[at])
        start(swapped.at[at], nears.at[at])
    for piece in range(PIECES):
        at = pl.ds(piece * rows, rows)
        start(mine.at[at], held.at[at])
        start(arrived.at[at], others.at[at])
    results = []

    def finish(source, target):
        results.append(pltpu.make_async_copy(source, target, out_sems.at[len(results)]))
        results[-1].start()

    for half, target in enumerate((out_a, out_b)):
        at = pl.ds(half * home_rows, home_rows)
        copies[2 * half].wait()
        copies[2 * half + 1].wait()
        near = jnp.where(core[0] == 1, nears[at, :].astype(f32), 0.0)
        homes[at, :] = (homes[at, :].astype(f32) + near).astype(bf16)
        finish(homes.at[at], target)
    for piece in range(PIECES):
        at = pl.ds(piece * rows, rows)
        copies[4 + 2 * piece].wait()
        copies[5 + 2 * piece].wait()
        held[at, :] = (held[at, :].astype(f32) + others[at, :].astype(f32)).astype(bf16)
        finish(held.at[at], total.at[at])
    for copy in results:
        copy.wait()


def pair_call(core, *operands):
    half = (HALF_BLOCKS * WIDTH, HEAD_DIM)
    home = (ROWS, WIDTH)
    return pl.pallas_call(
        pair_kernel,
        in_specs=[SMEM] + [ANY] * 4,
        out_specs=[ANY] * 3,
        out_shape=[jax.ShapeDtypeStruct(shape, bf16) for shape in (half, (ROWS // 2, WIDTH), (ROWS // 2, WIDTH))],
        scratch_shapes=[pltpu.VMEM(shape, bf16) for shape in (half, half, home, home)]
        + [pltpu.SemaphoreType.DMA((4 + 2 * PIECES,)), pltpu.SemaphoreType.DMA((2 + PIECES,))],
        compiler_params=pltpu.CompilerParams(vmem_limit_bytes=62 * MIB),
        name="pair_sum",
    )(core, *operands)


def chips_kernel(parts, *refs):
    totals = refs[-1]
    total = jnp.sum(parts[...].astype(f32), axis=0, keepdims=True).astype(bf16)
    totals[...] = jnp.broadcast_to(total, totals.shape)


def chips_call(parts, *after):
    return pl.pallas_call(
        chips_kernel,
        in_specs=[VMEM] + [ANY] * len(after),
        out_specs=VMEM,
        out_shape=jax.ShapeDtypeStruct(parts.shape, bf16),
        compiler_params=pltpu.CompilerParams(vmem_limit_bytes=24 * MIB),
        name="chip_sum",
    )(parts, *after)


def unpack_kernel(flip, core, blocks, *refs):
    grad_w_in, grad_w_out, staging, sems = refs[-4:]
    for half in range(2):

        @pl.when(core[0] == half ^ flip)
        def _(half=half):
            copies = []
            for at in range(HALF_BLOCKS):
                staging[at] = blocks[at].astype(f32)
                block = half * HALF_BLOCKS + at
                if block < 4 * HEADS:
                    target = grad_w_in.at[:, pl.ds(block * HEAD_DIM, HEAD_DIM)]
                else:
                    target = grad_w_out.at[:, pl.ds((block - 4 * HEADS) * HEAD_DIM, HEAD_DIM)]
                copies.append(pltpu.make_async_copy(staging.at[at], target, sems.at[at]))
                copies[-1].start()
            for copy in copies:
                copy.wait()


def unpack_call(core, blocks, flip, into=()):
    return pl.pallas_call(
        functools.partial(unpack_kernel, flip),
        in_specs=[SMEM, VMEM] + [ANY] * len(into),
        out_specs=[ANY] * 2,
        out_shape=(
            jax.ShapeDtypeStruct((WIDTH, 4 * WIDTH), f32),
            jax.ShapeDtypeStruct((WIDTH, WIDTH), f32),
        ),
        scratch_shapes=[
            pltpu.VMEM((HALF_BLOCKS, WIDTH, HEAD_DIM), f32),
            pltpu.SemaphoreType.DMA((HALF_BLOCKS,)),
        ],
        input_output_aliases={2: 0, 3: 1} if into else {},
        compiler_params=pltpu.CompilerParams(vmem_limit_bytes=24 * MIB),
        cost_estimate=pl.CostEstimate(flops=4 * 10**9, bytes_accessed=4 * MIB, transcendentals=0),
        name="unpack",
    )(core, blocks, *into)


def step_kernel(
    core, in_gain, tokens, cotangent, grad_normed, sent_a, sent_b, swapped, after, grad_tokens,
    rows_in, cot, grad, sent, near, result, sems, out_sems,
):
    del after
    half = ROWS // 2
    copies = []
    for part, sent_half in enumerate((sent_a, sent_b)):
        at = pl.ds(part * half, half)
        for source, target in (
            (tokens.at[at], rows_in.at[at]),
            (grad_normed.at[at], grad.at[at]),
            (swapped.at[at], near.at[at]),
            (sent_half, sent.at[at]),
            (cotangent.at[at], cot.at[at]),
        ):
            copies.append(pltpu.make_async_copy(source, target, sems.at[len(copies)]))
            copies[-1].start()
    results = []
    for part in range(2):
        at = pl.ds(part * half, half)
        copies[5 * part].wait()
        normed, inverse = layer_norm_rows(rows_in[at, :].astype(f32))
        for copy in copies[5 * part + 1 : 5 * part + 5]:
            copy.wait()
        home = jnp.where(core[0] == 0, near[at, :].astype(f32), 0.0)
        scaled_grad = (grad[at, :] + sent[at, :].astype(f32) + home) * in_gain[...]
        first = jnp.mean(scaled_grad, axis=1, keepdims=True)
        second = jnp.mean(scaled_grad * normed, axis=1, keepdims=True)
        result[at, :] = (
            cot[at, :].astype(f32) + (scaled_grad - first - normed * second) * inverse
        ).astype(bf16)
        results.append(pltpu.make_async_copy(result.at[at], grad_tokens.at[at], out_sems.at[part]))
        results[-1].start()
    for copy in results:
        copy.wait()


def step_call(*operands):
    shape = (ROWS, WIDTH)
    return pl.pallas_call(
        step_kernel,
        in_specs=[SMEM, VMEM] + [ANY] * 7,
        out_specs=ANY,
        out_shape=jax.ShapeDtypeStruct(shape, bf16),
        scratch_shapes=[pltpu.VMEM(shape, kind) for kind in (bf16, bf16, f32, bf16, bf16, bf16)]
        + [pltpu.SemaphoreType.DMA((10,)), pltpu.SemaphoreType.DMA((2,))],
        compiler_params=pltpu.CompilerParams(vmem_limit_bytes=62 * MIB),
        name="input_norm_gradient",
    )(*operands)


def shifted(value, steps):
    count = 128
    first, last = (max(0, -steps), min(count, count - steps))
    return lax.ppermute(value, ALL, [(source, source + steps) for source in range(first, last)])


SWAP = [(0, 1), (1, 0)]


def on_device(tokens, user_ids, in_gain, out_gain, w_in, w_out, cotangent):
    core = lax.axis_index("core").astype(jnp.int32).reshape(1)
    in_gain_row = in_gain.reshape(1, WIDTH)
    own_ids = user_ids.reshape(1, ROWS)

    far = shifted(tokens, 2)
    near_a = lax.ppermute(tokens, "core", [(0, 1)])
    far_ids = shifted(own_ids, 2)
    near_ids = shifted(own_ids, 1)
    *window, uq_t, uq_slope_t = own_call(tokens, in_gain_row, w_in)
    far = relay_call(far, uq_t, far_ids, near_ids)
    near_b = lax.ppermute(far, "core", [(1, 0)])
    normed_t, kv, kv_t, kv_slope = window
    layer_out, grad_kv_pre, grad_uq_pre, far_grad, near_grad, mine, theirs = main_call(
        core, in_gain_row, out_gain.reshape(1, WIDTH), far_ids, near_ids, own_ids,
        far, near_a, near_b, w_in, kv, uq_t, kv_t, uq_slope_t, w_out, cotangent, tokens, normed_t, kv_slope,
    )

    arrived = lax.ppermute(theirs, "core", SWAP)
    swapped = lax.ppermute(near_grad, "core", SWAP)
    flat = (HALF_BLOCKS * WIDTH, HEAD_DIM)
    partial, out_a, out_b = pair_call(core, mine.reshape(flat), arrived.reshape(flat), far_grad, swapped)
    sent_a = slow_relay_call(shifted(out_a, -2))
    grad_normed = back_call(grad_kv_pre, grad_uq_pre, w_in, out_b)
    parts = lax.all_to_all(partial.reshape(64, 80, HEAD_DIM), CHIPS, 0, 0, tiled=True)
    totals = lax.all_to_all(chips_call(parts, grad_normed, sent_a), CHIPS, 0, 0, tiled=True)
    totals = totals.reshape(HALF_BLOCKS, WIDTH, HEAD_DIM)
    other = lax.ppermute(totals, "core", SWAP)
    halves = unpack_call(core, totals, 0)
    sent_b = slow_relay_call(shifted(out_b, -2), halves[1])
    grad_w_in, grad_w_out = unpack_call(core, other, 1, halves)
    grad_tokens = step_call(
        core, in_gain_row, tokens, cotangent, grad_normed, sent_a, sent_b, swapped, grad_w_out,
    )
    return (layer_out, grad_tokens, grad_w_in, grad_w_out)


def solution(mesh):
    fine = Mesh(mesh.devices.reshape(2, 4, 2, 4, 2), ALL)
    placed = (P(ALL, None), P(ALL), P(), P(), P(), P(), P(ALL, None))
    return jax.shard_map(
        on_device,
        mesh=fine,
        in_specs=placed,
        out_specs=(P(ALL, None), P(ALL, None), P(), P()),
        check_vma=False,
    )
```
